512 devices in a mesh: batch: 16 (over z, core), ctx: 32 (over y, x).
Axes of the slice: x: 4, y: 8, z: 8, core: 2. Of those that a mesh axis runs over, the one named last changes fastest.
Arguments:
- q_latent: bfloat16 [4, 32, 64, 512], P(None, 'ctx', 'batch'), may hold values from -48 to 48
- q_rope: bfloat16 [4, 32, 64, 64], P(None, 'ctx', 'batch'), may hold values from -3 to 3
- cache_latent: bfloat16 [32, 32768, 512], P('batch', 'ctx'), may hold values from -6 to 6, as said below
- cache_rope: bfloat16 [32, 32768, 64], P('batch', 'ctx'), may hold values from -6 to 6
- new_latent: bfloat16 [4, 32, 512], P(None, 'batch'), may hold values from -6 to 6, as said below
- new_rope: bfloat16 [4, 32, 64], P(None, 'batch'), may hold values from -6 to 6
- lengths: int32 [32], P('batch'), may hold values from 8192 to 32768, as said below
- selected: int32 [4, 32, 8, 3], P(None, 'batch'), may hold values from 0 to 63, as said below
- w_uv: bfloat16 [64, 512, 128], P('batch'), may hold values from -2 to 2
Outputs:
- attended: bfloat16 [4, 32, 64, 128], P(None, None, 'batch')
The draws below stay inside these ranges and needn't reach their ends.
Inputs may be any that keep to these rules, and one draw needn't show every extreme that they name: `lengths`: filled positions of one request; one request is full and one holds exactly 8192. `selected`: the 3 ids of one row are distinct block ids, each below ceil(lengths[r] / 512); every row holds block 0 and the request's last filled block. `new_latent`: Real-valued latent entries. `cache_latent`: Real-valued latent entries.
All inputs are finite; a program needn't handle non-finite values.
Results may differ from the reference program's by a relative error of at most 0.0059.
Values may be sent and summed in bfloat16 or wider, within the bound.
A program may use at most 128 MiB of HBM per device.

```python
import jax
import jax.numpy as jnp
from jax import lax

H = 64
KL = 512
KR = 64
VH = 128
BLOCK = 512
TOPK = 3
GROUPS = 8
STEPS = 4
REQ = 32
LEN = 32768


def shared_latent(key):
    return jnp.clip(jax.random.normal(key, (STEPS, REQ, KL), jnp.float32), -6.0, 6.0)


def shared_lengths(key):
    inner = jax.random.fold_in(key, 50)
    first_key, second_key = jax.random.split(inner)
    raw_lengths = jax.random.randint(first_key, (REQ,), LEN // 4, LEN + 1)
    order_perm = jax.random.permutation(second_key, REQ)
    raw_lengths = raw_lengths.at[order_perm[0]].set(LEN)
    raw_lengths = raw_lengths.at[order_perm[1]].set(LEN // 4)
    return raw_lengths.astype(jnp.int32)


def draw_new_latent(key, part):
    shared = shared_latent(key)
    return shared.astype(jnp.bfloat16)


def draw_q_latent(key, part):
    key = jax.random.fold_in(key, 2)
    base_key = jax.random.fold_in(key, 0)
    sharp_key = jax.random.fold_in(key, 4)
    level_key = jax.random.fold_in(key, 5)
    sharp_levels = jnp.array([6.0, 8.0], jnp.float32)
    sharp_factor = sharp_levels[jax.random.randint(level_key, (STEPS, REQ, H), 0, 2)]
    sharp_mask = jax.random.uniform(sharp_key, (STEPS, REQ, H), jnp.float32) < 1.0 / 8.0
    values = jnp.clip(jax.random.normal(base_key, (STEPS, REQ, H, KL), jnp.float32), -6.0, 6.0)
    values = values * jnp.where(sharp_mask, sharp_factor, 1.0)[..., None]
    return values.astype(jnp.bfloat16)


def draw_cache_latent(key, part):
    key = jax.random.fold_in(key, 5)
    base_key = jax.random.fold_in(key, 0)
    values = jnp.clip(jax.random.normal(base_key, (REQ, LEN, KL), jnp.float32), -6.0, 6.0)
    return values.astype(jnp.bfloat16)


def draw_lengths(key, part):
    raw_lengths = shared_lengths(key)
    return raw_lengths


def draw_selected(key, part):
    raw_lengths = shared_lengths(key)
    key = jax.random.fold_in(key, 4)
    block_count = LEN // BLOCK
    filled = (raw_lengths + BLOCK - 1) // BLOCK
    index_row = jnp.arange(block_count, dtype=jnp.int32)
    noise_draw = jax.random.randint(key, (STEPS, REQ, GROUPS, block_count), 0, 2 * block_count)
    ranking = (noise_draw + index_row) * block_count + index_row
    last_block = (filled - 1)[None, :, None, None]
    ranking = jnp.where(index_row == 0, 4 * block_count * block_count - 1, ranking)
    ranking = jnp.where(index_row == last_block, 4 * block_count * block_count, ranking)
    ranking = jnp.where(index_row > last_block, -1, ranking)
    chosen = jax.lax.top_k(ranking, TOPK)[1]
    return chosen.astype(jnp.int32)


def shard_levels(stream_key, extent, cuts, low, largest):
    level, own = 1.0, jax.random.fold_in(stream_key, 6)
    for dim, shards_of in cuts:
        draws = jnp.exp(jax.random.uniform(jax.random.fold_in(own, dim), (shards_of,), jnp.float32, low / len(cuts), largest / len(cuts)))
        level = level * jnp.repeat(draws, extent[dim] // shards_of).reshape([-1 if axis == dim else 1 for axis in range(len(extent))])
    return level


def bell_draw(own_key, dims, deviation, limit, cuts=(), held_as=jnp.bfloat16):
    gain = shard_levels(own_key, dims, cuts, -0.22, 0.18) if cuts else 1.0
    values = jax.random.normal(own_key, dims, jnp.float32) * deviation * gain
    return jnp.minimum(jnp.maximum(values, -limit), limit).astype(held_as)


def setup_inputs(seed: int = 0) -> dict:
    seeds = jax.random.split(jax.random.key(seed), 10)
    return {
        "q_latent": draw_q_latent(jax.random.fold_in(seeds[9], 71), 0),
        "q_rope": bell_draw(seeds[1], (STEPS, REQ, H, KR), 0.5, 3.0, ((1, 32), (2, 16))),
        "cache_latent": draw_cache_latent(jax.random.fold_in(seeds[9], 71), 0),
        "cache_rope": bell_draw(seeds[3], (REQ, LEN, KR), 1.0, 6.0, ((0, 16), (1, 32))),
        "new_latent": draw_new_latent(jax.random.fold_in(seeds[9], 71), 0),
        "new_rope": bell_draw(seeds[5], (STEPS, REQ, KR), 1.0, 6.0, ((1, 16),)),
        "lengths": draw_lengths(jax.random.fold_in(seeds[9], 71), 0),
        "selected": draw_selected(jax.random.fold_in(seeds[9], 71), 0),
        "w_uv": bell_draw(seeds[8], (H, KL, VH), (KL // 64) ** -0.5, 2.0, ((0, 16),)),
    }


def one_request(pieces):
    q_lat, q_rot, lat_cache, rot_cache, new_lat, new_rot, length, chosen_ids = pieces
    step_count, head_count, row_width = q_lat.shape
    groups = chosen_ids.shape[1]
    per_group = head_count // groups
    topk_count = chosen_ids.shape[2]
    rot_width = rot_cache.shape[-1]
    scale = (VH + KR) ** -0.5
    lat_blocks = lat_cache.reshape(-1, BLOCK, row_width)[chosen_ids]
    lat_blocks = lat_blocks.reshape(step_count, groups, topk_count * BLOCK, row_width).astype(jnp.float32)
    rot_blocks = rot_cache.reshape(-1, BLOCK, rot_width)[chosen_ids]
    rot_blocks = rot_blocks.reshape(step_count, groups, topk_count * BLOCK, rot_width).astype(jnp.float32)
    position = chosen_ids[..., None].astype(jnp.int32) * BLOCK + jnp.arange(BLOCK, dtype=jnp.int32)
    position = position.reshape(step_count, groups, topk_count * BLOCK)
    valid_mask = (position < length)[:, :, None, :]
    lat_query = q_lat.astype(jnp.float32).reshape(step_count, groups, per_group, row_width)
    rot_query = q_rot.astype(jnp.float32).reshape(step_count, groups, per_group, rot_width)
    scores = jnp.einsum('sghd,sgjd->sghj', lat_query, lat_blocks)
    scores = (scores + jnp.einsum('sghd,sgjd->sghj', rot_query, rot_blocks)) * scale
    new_scores = jnp.einsum('shd,ud->shu', q_lat.astype(jnp.float32), new_lat.astype(jnp.float32))
    new_scores = (new_scores + jnp.einsum('shd,ud->shu', q_rot.astype(jnp.float32), new_rot.astype(jnp.float32))) * scale
    causal = (jnp.arange(step_count)[:, None] >= jnp.arange(step_count)[None, :])[:, None, :]
    cache_top = jnp.max(jnp.where(valid_mask, scores, -jnp.inf), axis=-1).reshape(step_count, head_count)
    new_top = jnp.max(jnp.where(causal, new_scores, -jnp.inf), axis=-1)
    row_top = jnp.maximum(cache_top, new_top)
    weights = jnp.where(valid_mask, jnp.exp(scores - row_top.reshape(step_count, groups, per_group)[..., None]), 0.0)
    new_weights = jnp.where(causal, jnp.exp(new_scores - row_top[..., None]), 0.0)
    total_sum = jnp.sum(weights, axis=-1).reshape(step_count, head_count) + jnp.sum(new_weights, axis=-1)
    rounded = lax.optimization_barrier(weights.astype(jnp.bfloat16)).astype(jnp.float32)
    new_rounded = lax.optimization_barrier(new_weights.astype(jnp.bfloat16)).astype(jnp.float32)
    mixed_sum = jnp.einsum('sghj,sgjd->sghd', rounded, lat_blocks).reshape(step_count, head_count, row_width)
    mixed_sum = mixed_sum + jnp.einsum('shu,ud->shd', new_rounded, new_lat.astype(jnp.float32))
    return mixed_sum / total_sum[..., None]


def reference(q_latent, q_rope, cache_latent, cache_rope, new_latent, new_rope, lengths, selected, w_uv):
    pieces = (jnp.transpose(q_latent, (1, 0, 2, 3)), jnp.transpose(q_rope, (1, 0, 2, 3)),
              cache_latent, cache_rope,
              jnp.transpose(new_latent, (1, 0, 2)), jnp.transpose(new_rope, (1, 0, 2)),
              lengths, jnp.transpose(selected, (1, 0, 2, 3)))
    latent_out = lax.map(one_request, pieces)
    attended = jnp.einsum('rshd,hdv->srhv', latent_out, w_uv.astype(jnp.float32), precision=lax.Precision.HIGHEST)
    return attended.astype(jnp.bfloat16)
```

```python
import functools

import jax
import jax.numpy as jnp
from jax import lax
from jax.experimental import pallas as pl
from jax.experimental.pallas import tpu as pltpu
from jax.sharding import PartitionSpec as P

MESH = pl.DeviceIdType.MESH
KL = 512
KR = 64
VH = 128
BLOCK = 512
STEPS = 4
NX = 4
LOCAL_HEADS = 4
ROWS = STEPS * LOCAL_HEADS
WIDE = KL + 128
SCALE = (VH + KR) ** (-0.5)
NEG = -1e30
LAST = (((1,), (1,)), ((), ()))
FIRST = (((1,), (0,)), ((), ()))


def column(x, core):
    source_core = (x // 2 + core) % 2
    source_x = x + source_core * (NX - 1 - 2 * x)
    request = source_x % 2
    return request, source_core, source_x


def packed(out, top, total):
    lane = lax.broadcasted_iota(jnp.int32, (out.shape[0], 128), 1)
    high = total.astype(jnp.bfloat16).astype(jnp.float32)
    stats = jnp.where(lane == 0, top, jnp.where(lane == 1, high, jnp.where(lane == 2, total - high, 0.0)))
    return jnp.concatenate([out.astype(jnp.bfloat16), stats.astype(jnp.bfloat16)], axis=1)


def merged(parts, top):
    stats = [part[:, KL:].astype(jnp.float32) for part in parts]
    for stat in stats:
        top = stat[:, 0:1] if top is None else jnp.maximum(top, stat[:, 0:1])
    out, total = None, None
    for part, stat in zip(parts, stats):
        factor = jnp.exp(stat[:, 0:1] - top)
        share = factor * (stat[:, 1:2] + stat[:, 2:3])
        term = factor * part[:, :KL].astype(jnp.float32)
        out = term if out is None else out + term
        total = share if total is None else total + share
    return out, top, total


def kernel(
    n,
    length_ref, ql_ref, qr_ref, sel_ref, nl_ref, nr_ref, lat_hbm, rope_hbm, w_hbm,
    out_ref,
    lat, rope, w, rows32, mine, q_all, keep, part, part_in, joint, joint_in, done, done_in, gathered,
    local_sem, perm_sem, y_send, y_recv, x_send, x_recv, px_send, px_recv, py_send, py_recv,
    back_sem, oy_send, oy_recv, ox_send, ox_recv,
):
    b, c = lax.axis_index("batch"), lax.axis_index("ctx")
    z, core = b // 2, b % 2
    y, x = c // NX, c % NX
    half = n // 2

    loads = [
        pltpu.make_async_copy(src, dst, local_sem.at[k])
        for k, (src, dst) in enumerate(((lat_hbm, lat), (rope_hbm, rope), (w_hbm, w)))
    ]
    for load in loads:
        load.start()

    def at_y(step):
        return (b, ((y + step + n) % n) * NX + x)

    def at_x(step):
        return (b, y * NX + (x + step + NX) % NX)

    request, source_core, source_x = column(x, core)
    own = request * 2 + source_core
    origin = (((y + half) % n) * 2 + source_core, z * NX + source_x)
    goal_x = x + core * (NX - 1 - 2 * x)
    goal = (y * 2 + x // 2, ((z + half) % n) * NX + goal_x)
    goal_slot = (x % 2) * 2 + core

    barrier = pltpu.get_barrier_semaphore()

    @pl.loop(1, n)
    def _(d):
        pl.semaphore_signal(barrier, inc=1, device_id=at_y(d), device_id_type=MESH)

    @pl.loop(1, NX)
    def _(d):
        pl.semaphore_signal(barrier, inc=1, device_id=at_x(d), device_id_type=MESH)

    pl.semaphore_signal(barrier, inc=1, device_id=goal, device_id_type=MESH)
    pl.semaphore_signal(barrier, inc=1, device_id=origin, device_id_type=MESH)

    for t in range(STEPS):
        span = pl.ds(t * LOCAL_HEADS, LOCAL_HEADS)
        rows32[span, :KL] = ql_ref[t, 0].astype(jnp.float32)
        rows32[span, KL:KL + KR] = qr_ref[t, 0].astype(jnp.float32)
    rows32[:, KL + KR:] = jnp.zeros((ROWS, WIDE - KL - KR), jnp.float32)
    mine[...] = rows32[...].astype(jnp.bfloat16)

    pl.semaphore_wait(barrier, n - 1 + NX - 1 + 2)

    def remote(src, dst, send, recv, device):
        return pltpu.make_async_remote_copy(
            src_ref=src, dst_ref=dst, send_sem=send, recv_sem=recv, device_id=device, device_id_type=MESH
        )

    permute = remote(mine, q_all.at[goal_slot, (z + half) % n], perm_sem.at[0], perm_sem.at[1], goal)
    permute.start()

    tall = n * ROWS
    row = lax.broadcasted_iota(jnp.int32, (tall, STEPS * n), 0)
    unit = lax.broadcasted_iota(jnp.int32, (tall, STEPS * n), 1)
    group = (row // ROWS + half) % n
    step = (row % ROWS) // LOCAL_HEADS
    spread = jnp.where(unit == step * n + group, 1.0, 0.0).astype(jnp.bfloat16)
    lane = lax.broadcasted_iota(jnp.int32, (STEPS * n, 128), 1)
    for r in range(2):
        chosen = jnp.concatenate([sel_ref[t, r] for t in range(STEPS)], axis=0)
        hits = [
            jnp.max(jnp.where(chosen == c * 2 + k, 1.0, 0.0), axis=1, keepdims=True) for k in range(2)
        ]
        table = jnp.where(lane == 0, hits[0], jnp.where(lane == 1, hits[1], 0.0)).astype(jnp.bfloat16)
        keep[r] = lax.dot_general(spread, table, FIRST, preferred_element_type=jnp.float32)

    permute.wait_recv()

    def y_copy(d):
        slot = q_all.at[own, y]
        return remote(slot, slot, y_send.at[d - 1], y_recv.at[d - 1], at_y(d))

    def x_copy(d, e):
        slot = q_all.at[own, (y - e + n) % n]
        return remote(slot, slot, x_send.at[d - 1, e], x_recv.at[d - 1, e], at_x(d))

    @pl.loop(1, n)
    def _(s):
        y_copy(s % 2 * ((s + 1) // 2) + (1 - s % 2) * (n - s // 2)).start()

    for d in (1, 3, 2):
        x_copy(d, 0).start()

    q_own = q_all[own, y].astype(jnp.float32)
    row_step = lax.broadcasted_iota(jnp.int32, (ROWS, 1), 0) // LOCAL_HEADS
    second = request.astype(jnp.float32)
    new_rows, new_scores = [], []
    for u in range(STEPS):
        both = nl_ref[u].astype(jnp.float32)
        both_rope = nr_ref[u].astype(jnp.float32)
        new_row = both[0:1] * (1.0 - second) + both[1:2] * second
        new_rope = both_rope[0:1] * (1.0 - second) + both_rope[1:2] * second
        score = jnp.sum(q_own[:, :KL] * new_row, axis=1, keepdims=True)
        score = (score + jnp.sum(q_own[:, KL:KL + KR] * new_rope, axis=1, keepdims=True)) * SCALE
        new_rows.append(new_row)
        new_scores.append(jnp.where(row_step >= u, score, NEG))

    @pl.loop(1, n)
    def _(s):
        e = s % 2 * ((s + 1) // 2) + (1 - s % 2) * (n - s // 2)
        y_copy(e).wait_recv()
        for d in (1, 3, 2):
            x_copy(d, e).start()

    loads[0].wait()
    loads[1].wait()

    def px_copy(d):
        return remote(part.at[d], part_in.at[d - 1], px_send.at[d - 1], px_recv.at[d - 1], at_x(-d))

    @pl.loop(0, NX)
    def _(s):
        d = s + (s // 2) * (5 - 2 * s)
        r, from_core, _ = column((x - d + NX) % NX, core)

        @pl.when(d > 0)
        def _():
            @pl.loop(0, n)
            def _(e):
                x_copy(d, e).wait_recv()

        query = q_all[r * 2 + from_core].reshape(tall, WIDE)
        scores = lax.dot_general(query[:, :KL], lat[r], LAST, preferred_element_type=jnp.float32)
        scores = scores + lax.dot_general(
            query[:, KL:KL + KR], rope[r], LAST, preferred_element_type=jnp.float32
        )
        scores = scores * SCALE
        length = length_ref[r]
        hits = keep[r]
        place = lax.broadcasted_iota(jnp.int32, (tall, BLOCK), 1)
        masks, masked = [], []
        for k in range(2):
            mask = (hits[:, k:k + 1] > 0.5) & (place + (c * 2 + k) * BLOCK < length)
            masks.append(mask)
            masked.append(jnp.where(mask, scores[:, k * BLOCK:(k + 1) * BLOCK], NEG))
        top = jnp.maximum(
            jnp.max(masked[0], axis=1, keepdims=True), jnp.max(masked[1], axis=1, keepdims=True)
        )
        top = top.astype(jnp.bfloat16).astype(jnp.float32)
        weights = [jnp.where(m, jnp.exp(v - top), 0.0) for m, v in zip(masks, masked)]
        total = jnp.sum(weights[0], axis=1, keepdims=True) + jnp.sum(weights[1], axis=1, keepdims=True)
        rounded = jnp.concatenate([v.astype(jnp.bfloat16) for v in weights], axis=1)
        out = lax.dot_general(rounded, lat[r], FIRST, preferred_element_type=jnp.float32)
        part[d] = packed(out, top, total).reshape(n, ROWS, WIDE)

        @pl.when(d > 0)
        def _():
            px_copy(d).start()

    for d in (1, 3, 2):
        px_copy(d).wait_recv()
    parts = [part[0]] + [part_in[k] for k in range(NX - 1)]
    out, top, total = merged([v.reshape(tall, WIDE) for v in parts], None)
    joint[...] = packed(out, top, total).reshape(n, ROWS, WIDE)

    def py_copy(d):
        return remote(
            joint.at[(y + d) % n], joint_in.at[d - 1], py_send.at[d - 1], py_recv.at[d - 1], at_y(d)
        )

    @pl.loop(1, n)
    def _(s):
        py_copy(s % 2 * ((s + 1) // 2) + (1 - s % 2) * (n - s // 2)).start()

    @pl.loop(1, n)
    def _(d):
        py_copy(d).wait_recv()

    new_top = new_scores[0]
    for score in new_scores[1:]:
        new_top = jnp.maximum(new_top, score)
    out, top, total = merged([joint[y]] + [joint_in[k] for k in range(n - 1)], new_top)
    for u in range(STEPS):
        weight = jnp.where(row_step >= u, jnp.exp(new_scores[u] - top), 0.0)
        total = total + weight
        out = out + weight.astype(jnp.bfloat16).astype(jnp.float32) * new_rows[u]
    done[...] = out / total

    back = remote(done, done_in, back_sem.at[0], back_sem.at[1], origin)
    back.start()
    loads[2].wait()
    back.wait_recv()
    value = done_in[...]
    high = value.astype(jnp.bfloat16)
    rest = value - high.astype(jnp.float32)
    middle = rest.astype(jnp.bfloat16)
    low = (rest - middle.astype(jnp.float32)).astype(jnp.bfloat16)
    terms = jnp.concatenate([high, middle, low], axis=0)
    row_head = lax.broadcasted_iota(jnp.int32, (ROWS, VH), 0) % LOCAL_HEADS
    result = jnp.zeros((ROWS, VH), jnp.float32)
    for h in range(LOCAL_HEADS):
        product = lax.dot_general(terms, w[h], FIRST, preferred_element_type=jnp.float32)
        product = product[:ROWS] + (product[ROWS:2 * ROWS] + product[2 * ROWS:])
        result = jnp.where(row_head == h, product, result)
    gathered[x, y] = result.astype(jnp.bfloat16)

    def oy_copy(d):
        slot = gathered.at[x, y]
        return remote(slot, slot, oy_send.at[d - 1], oy_recv.at[d - 1], at_y(d))

    def ox_copy(d):
        slot = gathered.at[x]
        return remote(slot, slot, ox_send.at[d - 1], ox_recv.at[d - 1], at_x(d))

    @pl.loop(1, n)
    def _(s):
        oy_copy(s % 2 * ((s + 1) // 2) + (1 - s % 2) * (n - s // 2)).start()

    @pl.loop(1, n)
    def _(d):
        oy_copy(d).wait_recv()

    for d in (1, 3, 2):
        ox_copy(d).start()
    for d in (1, 3, 2):
        ox_copy(d).wait_recv()
    out_ref[...] = gathered[...]

    permute.wait_send()
    back.wait_send()

    @pl.loop(1, n)
    def _(d):
        y_copy(d).wait_send()
        py_copy(d).wait_send()
        oy_copy(d).wait_send()

    @pl.loop(1, NX)
    def _(d):
        px_copy(d).wait_send()
        ox_copy(d).wait_send()

        @pl.loop(0, n)
        def _(e):
            x_copy(d, e).wait_send()


def local(
    q_latent, q_rope, cache_latent, cache_rope, new_latent, new_rope, lengths, selected, w_uv
):
    n = lax.axis_size("ctx") // NX
    held = cache_latent.shape[1]
    bf16, f32 = jnp.bfloat16, jnp.float32
    dma = pltpu.SemaphoreType.DMA
    vmem, anywhere = pl.BlockSpec(memory_space=pltpu.VMEM), pl.BlockSpec(memory_space=pl.ANY)
    out = pl.pallas_call(
        functools.partial(kernel, n),
        out_shape=jax.ShapeDtypeStruct((NX, n, ROWS, VH), bf16),
        in_specs=[pl.BlockSpec(memory_space=pltpu.SMEM)] + [vmem] * 5 + [anywhere] * 3,
        out_specs=vmem,
        scratch_shapes=[
            pltpu.VMEM((2, held, KL), bf16),
            pltpu.VMEM((2, held, KR), bf16),
            pltpu.VMEM((LOCAL_HEADS, KL, VH), bf16),
            pltpu.VMEM((ROWS, WIDE), f32),
            pltpu.VMEM((ROWS, WIDE), bf16),
            pltpu.VMEM((NX, n, ROWS, WIDE), bf16),
            pltpu.VMEM((2, n * ROWS, 128), f32),
            pltpu.VMEM((NX, n, ROWS, WIDE), bf16),
            pltpu.VMEM((NX - 1, n, ROWS, WIDE), bf16),
            pltpu.VMEM((n, ROWS, WIDE), bf16),
            pltpu.VMEM((n - 1, ROWS, WIDE), bf16),
            pltpu.VMEM((ROWS, KL), f32),
            pltpu.VMEM((ROWS, KL), f32),
            pltpu.VMEM((NX, n, ROWS, VH), bf16),
            dma((3,)),
            dma((2,)),
            dma((n - 1,)), dma((n - 1,)),
            dma((NX - 1, n)), dma((NX - 1, n)),
            dma((NX - 1,)), dma((NX - 1,)),
            dma((n - 1,)), dma((n - 1,)),
            dma((2,)),
            dma((n - 1,)), dma((n - 1,)),
            dma((NX - 1,)), dma((NX - 1,)),
        ],
        compiler_params=pltpu.CompilerParams(
            collective_id=0, has_side_effects=True, vmem_limit_bytes=40 * 1024 * 1024
        ),
    )(lengths, q_latent, q_rope, selected, new_latent, new_rope, cache_latent, cache_rope, w_uv)
    out = out.reshape(NX, n, STEPS, LOCAL_HEADS, VH)
    return jnp.transpose(out, (2, 1, 0, 3, 4)).reshape(STEPS, NX * n, LOCAL_HEADS, VH)


def solution(mesh):
    placed = (
        P(None, "ctx", "batch", None),
        P(None, "ctx", "batch", None),
        P("batch", "ctx", None),
        P("batch", "ctx", None),
        P(None, "batch", None),
        P(None, "batch", None),
        P("batch"),
        P(None, "batch", None, None),
        P("batch", None, None),
    )
    return jax.shard_map(
        local, mesh=mesh, in_specs=placed, out_specs=P(None, None, "batch", None), check_vma=False
    )
```

```python
import functools

import jax
import jax.numpy as jnp
from jax import lax
from jax.experimental import pallas as pl
from jax.experimental.pallas import tpu as pltpu
from jax.sharding import PartitionSpec as P

MESH = pl.DeviceIdType.MESH
KL = 512
KR = 64
VH = 128
BLOCK = 512
STEPS = 4
NX = 4
LOCAL_HEADS = 4
ROWS = STEPS * LOCAL_HEADS
WIDE = KL + 128
SCALE = (VH + KR) ** (-0.5)
NEG = -1e30
LAST = (((1,), (1,)), ((), ()))
FIRST = (((1,), (0,)), ((), ()))


def column(x, core):
    source_core = (x // 2 + core) % 2
    source_x = x + source_core * (NX - 1 - 2 * x)
    request = source_x % 2
    return request, source_core, source_x


def packed(out, top, total):
    lane = lax.broadcasted_iota(jnp.int32, (out.shape[0], 128), 1)
    high = total.astype(jnp.bfloat16).astype(jnp.float32)
    stats = jnp.where(lane == 0, top, jnp.where(lane == 1, high, jnp.where(lane == 2, total - high, 0.0)))
    return jnp.concatenate([out.astype(jnp.bfloat16), stats.astype(jnp.bfloat16)], axis=1)


def merged(parts, top):
    stats = [part[:, KL:].astype(jnp.float32) for part in parts]
    for stat in stats:
        top = stat[:, 0:1] if top is None else jnp.maximum(top, stat[:, 0:1])
    out, total = None, None
    for part, stat in zip(parts, stats):
        factor = jnp.exp(stat[:, 0:1] - top)
        share = factor * (stat[:, 1:2] + stat[:, 2:3])
        term = factor * part[:, :KL].astype(jnp.float32)
        out = term if out is None else out + term
        total = share if total is None else total + share
    return out, top, total


def kernel(
    n,
    length_hbm, ql_hbm, qr_hbm, sel_hbm, nl_hbm, nr_hbm, lat_hbm, rope_hbm, w_hbm,
    out_ref,
    length_ref, ql_ref, qr_ref, sel_ref, nl_ref, nr_ref, lat, rope, w, rows32, mine, q_all, keep, part, part_in, joint, joint_in, done, done_in, gathered,
    local_sem, perm_sem, y_send, y_recv, x_send, x_recv, px_send, px_recv, py_send, py_recv,
    back_sem, oy_send, oy_recv, ox_send, ox_recv,
):
    b, c = lax.axis_index("batch"), lax.axis_index("ctx")
    z, core = b // 2, b % 2
    y, x = c // NX, c % NX
    half = n // 2

    pairs = (
        (ql_hbm, ql_ref), (qr_hbm, qr_ref), (sel_hbm, sel_ref), (nl_hbm, nl_ref), (nr_hbm, nr_ref),
        (length_hbm, length_ref), (lat_hbm, lat), (rope_hbm, rope), (w_hbm, w),
    )
    loads = [pltpu.make_async_copy(src, dst, local_sem.at[k]) for k, (src, dst) in enumerate(pairs)]
    for load in loads:
        load.start()

    def at_y(step):
        return (b, ((y + step + n) % n) * NX + x)

    def at_x(step):
        return (b, y * NX + (x + step + NX) % NX)

    request, source_core, source_x = column(x, core)
    own = request * 2 + source_core
    origin = (((y + half) % n) * 2 + source_core, z * NX + source_x)
    goal_x = x + core * (NX - 1 - 2 * x)
    goal = (y * 2 + x // 2, ((z + half) % n) * NX + goal_x)
    goal_slot = (x % 2) * 2 + core

    barrier = pltpu.get_barrier_semaphore()

    @pl.loop(1, n)
    def _(d):
        pl.semaphore_signal(barrier, inc=1, device_id=at_y(d), device_id_type=MESH)

    @pl.loop(1, NX)
    def _(d):
        pl.semaphore_signal(barrier, inc=1, device_id=at_x(d), device_id_type=MESH)

    pl.semaphore_signal(barrier, inc=1, device_id=goal, device_id_type=MESH)
    pl.semaphore_signal(barrier, inc=1, device_id=origin, device_id_type=MESH)

    loads[0].wait()
    loads[1].wait()
    for t in range(STEPS):
        span = pl.ds(t * LOCAL_HEADS, LOCAL_HEADS)
        rows32[span, :KL] = ql_ref[t, 0].astype(jnp.float32)
        rows32[span, KL:KL + KR] = qr_ref[t, 0].astype(jnp.float32)
    rows32[:, KL + KR:] = jnp.zeros((ROWS, WIDE - KL - KR), jnp.float32)
    mine[...] = rows32[...].astype(jnp.bfloat16)

    pl.semaphore_wait(barrier, n - 1 + NX - 1 + 2)

    def remote(src, dst, send, recv, device):
        return pltpu.make_async_remote_copy(
            src_ref=src, dst_ref=dst, send_sem=send, recv_sem=recv, device_id=device, device_id_type=MESH
        )

    permute = remote(mine, q_all.at[goal_slot, (z + half) % n], perm_sem.at[0], perm_sem.at[1], goal)
    permute.start()

    tall = n * ROWS
    row = lax.broadcasted_iota(jnp.int32, (tall, n), 0)
    group = lax.broadcasted_iota(jnp.int32, (tall, n), 1)
    spread = jnp.where(group == (row // ROWS + half) % n, 1.0, 0.0).astype(jnp.bfloat16)
    loads[2].wait()
    hits = []
    for t in range(STEPS):
        chosen = sel_ref[t]
        for k in range(2):
            hits.append(jnp.max(jnp.where(chosen == c * 2 + k, 1.0, 0.0), axis=0))
    table = jnp.concatenate(hits, axis=0).astype(jnp.bfloat16)
    marks = lax.dot_general(spread, table, LAST, preferred_element_type=jnp.float32)
    lane = lax.broadcasted_iota(jnp.int32, (tall, STEPS * 4), 1)
    step = lax.broadcasted_iota(jnp.int32, (tall, STEPS * 4), 0) % ROWS // LOCAL_HEADS
    marks = jnp.where(lane // 4 == step, marks, 0.0).astype(jnp.bfloat16)
    source = lax.broadcasted_iota(jnp.int32, (STEPS * 4, 128), 0) % 4
    target = lax.broadcasted_iota(jnp.int32, (STEPS * 4, 128), 1)
    for r in range(2):
        pick = jnp.where((target < 2) & (source == target * 2 + r), 1.0, 0.0).astype(jnp.bfloat16)
        keep[r] = lax.dot_general(marks, pick, FIRST, preferred_element_type=jnp.float32)

    permute.wait_recv()

    def y_copy(d):
        slot = q_all.at[own, y]
        return remote(slot, slot, y_send.at[d - 1], y_recv.at[d - 1], at_y(d))

    def x_copy(d, e):
        slot = q_all.at[own, (y - e + n) % n]
        return remote(slot, slot, x_send.at[d - 1, e], x_recv.at[d - 1, e], at_x(d))

    @pl.loop(1, n)
    def _(s):
        y_copy(s % 2 * ((s + 1) // 2) + (1 - s % 2) * (n - s // 2)).start()

    for d in (1, 3, 2):
        x_copy(d, 0).start()

    loads[3].wait()
    loads[4].wait()
    q_own = q_all[own, y].astype(jnp.float32)
    row_step = lax.broadcasted_iota(jnp.int32, (ROWS, 1), 0) // LOCAL_HEADS
    second = request.astype(jnp.float32)
    new_rows, new_scores = [], []
    for u in range(STEPS):
        both = nl_ref[u].astype(jnp.float32)
        both_rope = nr_ref[u].astype(jnp.float32)
        new_row = both[0:1] * (1.0 - second) + both[1:2] * second
        new_rope = both_rope[0:1] * (1.0 - second) + both_rope[1:2] * second
        score = jnp.sum(q_own[:, :KL] * new_row, axis=1, keepdims=True)
        score = (score + jnp.sum(q_own[:, KL:KL + KR] * new_rope, axis=1, keepdims=True)) * SCALE
        new_rows.append(new_row)
        new_scores.append(jnp.where(row_step >= u, score, NEG))

    @pl.loop(1, n)
    def _(s):
        e = s % 2 * ((s + 1) // 2) + (1 - s % 2) * (n - s // 2)
        y_copy(e).wait_recv()
        for d in (1, 3, 2):
            x_copy(d, e).start()

    for load in loads[5:8]:
        load.wait()

    def px_copy(d):
        return remote(part.at[d], part_in.at[d - 1], px_send.at[d - 1], px_recv.at[d - 1], at_x(-d))

    @pl.loop(0, NX)
    def _(s):
        d = s + (s // 2) * (5 - 2 * s)
        r, from_core, _ = column((x - d + NX) % NX, core)

        @pl.when(d > 0)
        def _():
            @pl.loop(0, n)
            def _(e):
                x_copy(d, e).wait_recv()

        query = q_all[r * 2 + from_core].reshape(tall, WIDE)
        scores = lax.dot_general(query[:, :KL], lat[r], LAST, preferred_element_type=jnp.float32)
        scores = scores + lax.dot_general(
            query[:, KL:KL + KR], rope[r], FIRST, preferred_element_type=jnp.float32
        )
        scores = scores * SCALE
        length = length_ref[r]
        hits = keep[r]
        place = lax.broadcasted_iota(jnp.int32, (tall, BLOCK), 1)
        masks, masked = [], []
        for k in range(2):
            mask = (hits[:, k:k + 1] > 0.5) & (place + (c * 2 + k) * BLOCK < length)
            masks.append(mask)
            masked.append(jnp.where(mask, scores[:, k * BLOCK:(k + 1) * BLOCK], NEG))
        top = jnp.maximum(
            jnp.max(masked[0], axis=1, keepdims=True), jnp.max(masked[1], axis=1, keepdims=True)
        )
        top = top.astype(jnp.bfloat16).astype(jnp.float32)
        weights = [jnp.where(m, jnp.exp(v - top), 0.0) for m, v in zip(masks, masked)]
        total = jnp.sum(weights[0], axis=1, keepdims=True) + jnp.sum(weights[1], axis=1, keepdims=True)
        rounded = jnp.concatenate([v.astype(jnp.bfloat16) for v in weights], axis=1)
        out = lax.dot_general(rounded, lat[r], FIRST, preferred_element_type=jnp.float32)
        part[d] = packed(out, top, total).reshape(n, ROWS, WIDE)

        @pl.when(d > 0)
        def _():
            px_copy(d).start()

    for d in (1, 3, 2):
        px_copy(d).wait_recv()
    parts = [part[0]] + [part_in[k] for k in range(NX - 1)]
    out, top, total = merged([v.reshape(tall, WIDE) for v in parts], None)
    joint[...] = packed(out, top, total).reshape(n, ROWS, WIDE)

    def py_copy(d):
        return remote(
            joint.at[(y + d) % n], joint_in.at[d - 1], py_send.at[d - 1], py_recv.at[d - 1], at_y(d)
        )

    @pl.loop(1, n)
    def _(s):
        py_copy(s % 2 * ((s + 1) // 2) + (1 - s % 2) * (n - s // 2)).start()

    @pl.loop(1, n)
    def _(d):
        py_copy(d).wait_recv()

    new_top = new_scores[0]
    for score in new_scores[1:]:
        new_top = jnp.maximum(new_top, score)
    out, top, total = merged([joint[y]] + [joint_in[k] for k in range(n - 1)], new_top)
    for u in range(STEPS):
        weight = jnp.where(row_step >= u, jnp.exp(new_scores[u] - top), 0.0)
        total = total + weight
        out = out + weight.astype(jnp.bfloat16).astype(jnp.float32) * new_rows[u]
    done[...] = out / total

    back = remote(done, done_in, back_sem.at[0], back_sem.at[1], origin)
    back.start()
    loads[8].wait()
    back.wait_recv()
    value = done_in[...]
    high = value.astype(jnp.bfloat16)
    rest = value - high.astype(jnp.float32)
    middle = rest.astype(jnp.bfloat16)
    low = (rest - middle.astype(jnp.float32)).astype(jnp.bfloat16)
    terms = jnp.concatenate([high, middle, low], axis=0)
    row_head = lax.broadcasted_iota(jnp.int32, (ROWS, VH), 0) % LOCAL_HEADS
    result = jnp.zeros((ROWS, VH), jnp.float32)
    for h in range(LOCAL_HEADS):
        product = lax.dot_general(terms, w[h], FIRST, preferred_element_type=jnp.float32)
        product = product[:ROWS] + (product[ROWS:2 * ROWS] + product[2 * ROWS:])
        result = jnp.where(row_head == h, product, result)
    gathered[x, y] = result.astype(jnp.bfloat16)

    def oy_copy(d):
        slot = gathered.at[x, y]
        return remote(slot, slot, oy_send.at[d - 1], oy_recv.at[d - 1], at_y(d))

    def ox_copy(d):
        slot = gathered.at[x]
        return remote(slot, slot, ox_send.at[d - 1], ox_recv.at[d - 1], at_x(d))

    @pl.loop(1, n)
    def _(s):
        oy_copy(s % 2 * ((s + 1) // 2) + (1 - s % 2) * (n - s // 2)).start()

    @pl.loop(1, n)
    def _(d):
        oy_copy(d).wait_recv()

    for d in (1, 3, 2):
        ox_copy(d).start()
    for d in (1, 3, 2):
        ox_copy(d).wait_recv()
    out_ref[...] = gathered[...]

    permute.wait_send()
    back.wait_send()

    @pl.loop(1, n)
    def _(d):
        y_copy(d).wait_send()
        py_copy(d).wait_send()
        oy_copy(d).wait_send()

    @pl.loop(1, NX)
    def _(d):
        px_copy(d).wait_send()
        ox_copy(d).wait_send()

        @pl.loop(0, n)
        def _(e):
            x_copy(d, e).wait_send()


def local(
    q_latent, q_rope, cache_latent, cache_rope, new_latent, new_rope, lengths, selected, w_uv
):
    n = lax.axis_size("ctx") // NX
    selected = jnp.transpose(selected, (0, 3, 1, 2))
    cache_rope = jnp.swapaxes(cache_rope, 1, 2)
    held = cache_latent.shape[1]
    bf16, f32 = jnp.bfloat16, jnp.float32
    dma = pltpu.SemaphoreType.DMA
    anywhere = pl.BlockSpec(memory_space=pl.ANY)
    out = pl.pallas_call(
        functools.partial(kernel, n),
        out_shape=jax.ShapeDtypeStruct((NX, n, ROWS, VH), bf16),
        in_specs=[anywhere] * 9,
        out_specs=pl.BlockSpec(memory_space=pltpu.VMEM),
        scratch_shapes=[
            pltpu.SMEM((2,), jnp.int32),
            pltpu.VMEM(q_latent.shape, bf16),
            pltpu.VMEM(q_rope.shape, bf16),
            pltpu.VMEM(selected.shape, jnp.int32),
            pltpu.VMEM(new_latent.shape, bf16),
            pltpu.VMEM(new_rope.shape, bf16),
            pltpu.VMEM((2, held, KL), bf16),
            pltpu.VMEM((2, KR, held), bf16),
            pltpu.VMEM((LOCAL_HEADS, KL, VH), bf16),
            pltpu.VMEM((ROWS, WIDE), f32),
            pltpu.VMEM((ROWS, WIDE), bf16),
            pltpu.VMEM((NX, n, ROWS, WIDE), bf16),
            pltpu.VMEM((2, n * ROWS, 128), f32),
            pltpu.VMEM((NX, n, ROWS, WIDE), bf16),
            pltpu.VMEM((NX - 1, n, ROWS, WIDE), bf16),
            pltpu.VMEM((n, ROWS, WIDE), bf16),
            pltpu.VMEM((n - 1, ROWS, WIDE), bf16),
            pltpu.VMEM((ROWS, KL), f32),
            pltpu.VMEM((ROWS, KL), f32),
            pltpu.VMEM((NX, n, ROWS, VH), bf16),
            dma((9,)),
            dma((2,)),
            dma((n - 1,)), dma((n - 1,)),
            dma((NX - 1, n)), dma((NX - 1, n)),
            dma((NX - 1,)), dma((NX - 1,)),
            dma((n - 1,)), dma((n - 1,)),
            dma((2,)),
            dma((n - 1,)), dma((n - 1,)),
            dma((NX - 1,)), dma((NX - 1,)),
        ],
        compiler_params=pltpu.CompilerParams(
            collective_id=0, has_side_effects=True, vmem_limit_bytes=60 * 1024 * 1024
        ),
    )(lengths, q_latent, q_rope, selected, new_latent, new_rope, cache_latent, cache_rope, w_uv)
    out = out.reshape(NX, n, STEPS, LOCAL_HEADS, VH)
    return jnp.transpose(out, (2, 1, 0, 3, 4)).reshape(STEPS, NX * n, LOCAL_HEADS, VH)


def solution(mesh):
    placed = (
        P(None, "ctx", "batch", None),
        P(None, "ctx", "batch", None),
        P("batch", "ctx", None),
        P("batch", "ctx", None),
        P(None, "batch", None),
        P(None, "batch", None),
        P("batch"),
        P(None, "batch", None, None),
        P("batch", None, None),
    )
    return jax.shard_map(
        local, mesh=mesh, in_specs=placed, out_specs=P(None, None, "batch", None), check_vma=False
    )
```

```python
import functools

import jax
import jax.numpy as jnp
from jax import lax
from jax.experimental import pallas as pl
from jax.experimental.pallas import tpu as pltpu
from jax.sharding import PartitionSpec as P

MESH = pl.DeviceIdType.MESH
KL = 512
KR = 64
VH = 128
BLOCK = 512
STEPS = 4
NX = 4
LOCAL_HEADS = 4
ROWS = STEPS * LOCAL_HEADS
WIDE = KL + 128
SCALE = (VH + KR) ** (-0.5)
NEG = -1e30
LAST = (((1,), (1,)), ((), ()))
FIRST = (((1,), (0,)), ((), ()))


def column(x, core):
    source_core = (x // 2 + core) % 2
    source_x = x + source_core * (NX - 1 - 2 * x)
    request = source_x % 2
    return request, source_core, source_x


def packed(out, top, total):
    lane = lax.broadcasted_iota(jnp.int32, (out.shape[0], 128), 1)
    high = total.astype(jnp.bfloat16).astype(jnp.float32)
    stats = jnp.where(lane == 0, top, jnp.where(lane == 1, high, jnp.where(lane == 2, total - high, 0.0)))
    return jnp.concatenate([out.astype(jnp.bfloat16), stats.astype(jnp.bfloat16)], axis=1)


def merged(parts, top):
    stats = [part[:, KL:].astype(jnp.float32)[:, :3] for part in parts]
    return joined([part[:, :KL] for part in parts], stats, top)


def joined(values, stats, top):
    for stat in stats:
        top = stat[:, 0:1] if top is None else jnp.maximum(top, stat[:, 0:1])
    out, total = None, None
    for value, stat in zip(values, stats):
        factor = jnp.exp(stat[:, 0:1] - top)
        share = factor * (stat[:, 1:2] + stat[:, 2:3])
        term = factor * value.astype(jnp.float32)
        out = term if out is None else out + term
        total = share if total is None else total + share
    return out, top, total


def kernel(
    n,
    length_hbm, ql_hbm, qr_hbm, sel_hbm, nl_hbm, nr_hbm, lat_hbm, rope_hbm, w_hbm,
    out_ref,
    length_ref, ql_ref, qr_ref, sel_ref, nl_ref, nr_ref, lat, rope, w, rows32, mine, q_all, keep,
    part, part_in, joint, joint_in, done, done_in, gathered,
    local_sem, q_send, q_recv, x_send, x_recv, px_send, px_recv, py_send, py_recv, back_sem,
    oy_send, oy_recv, ox_send, ox_recv,
):
    b, c = lax.axis_index("batch"), lax.axis_index("ctx")
    z, core = b // 2, b % 2
    y, x = c // NX, c % NX
    far = n // 2

    pairs = (
        (ql_hbm, ql_ref), (qr_hbm, qr_ref), (sel_hbm, sel_ref), (nl_hbm, nl_ref), (nr_hbm, nr_ref),
        (length_hbm, length_ref), (lat_hbm, lat), (rope_hbm, rope), (w_hbm, w),
    )
    loads = [pltpu.make_async_copy(src, dst, local_sem.at[k]) for k, (src, dst) in enumerate(pairs)]
    for load in loads:
        load.start()

    def at_y(step):
        return (b, ((y + step + n) % n) * NX + x)

    def at_x(step):
        return (b, y * NX + (x + step + NX) % NX)

    request, source_core, source_x = column(x, core)
    own = request * 2 + source_core
    goal_x = x + core * (NX - 1 - 2 * x)
    goal_column = (x % 2) * 2 + core
    itself = (y == z) & (x // 2 == core) & (goal_x == x)
    other = jnp.logical_not(itself)

    def goal(step):
        return (y * 2 + x // 2, ((y + step) % n) * NX + goal_x)

    def origin(step):
        return (((z + step) % n) * 2 + source_core, z * NX + source_x)

    barrier = pltpu.get_barrier_semaphore()

    def greet(device):
        pl.semaphore_signal(barrier, inc=1, device_id=device, device_id_type=MESH)

    @pl.loop(1, n)
    def _(d):
        greet(goal(d))
        greet(origin(d))
        greet(at_y(d))

    @pl.loop(1, NX)
    def _(d):
        greet(at_x(d))

    @pl.when(other)
    def _():
        greet(goal(0))
        greet(origin(0))

    loads[0].wait()
    loads[1].wait()
    for t in range(STEPS):
        span = pl.ds(t * LOCAL_HEADS, LOCAL_HEADS)
        rows32[span, :KL] = ql_ref[t, 0].astype(jnp.float32)
        rows32[span, KL:KL + KR] = qr_ref[t, 0].astype(jnp.float32)
    rows32[:, KL + KR:] = jnp.zeros((ROWS, WIDE - KL - KR), jnp.float32)
    mine[...] = rows32[...].astype(jnp.bfloat16)

    pl.semaphore_wait(barrier, 3 * (n - 1) + NX - 1 + 2 * other.astype(jnp.int32))

    def remote(src, dst, send, recv, device):
        return pltpu.make_async_remote_copy(
            src_ref=src, dst_ref=dst, send_sem=send, recv_sem=recv, device_id=device, device_id_type=MESH
        )

    def nearest(s):
        return s % 2 * ((s + 1) // 2) + (1 - s % 2) * ((n - s // 2) % n)

    def q_copy(d):
        return remote(mine, q_all.at[goal_column, z], q_send.at[d], q_recv.at[z], goal(d))

    def q_wait(k):
        slot = q_all.at[own, k]
        remote(slot, slot, q_send.at[0], q_recv.at[k], goal(0)).wait_recv()

    @pl.loop(1, n)
    def _(s):
        q_copy(nearest(n - s)).start()

    @pl.when(other)
    def _():
        q_copy(0).start()

    @pl.when(itself)
    def _():
        q_all[own, z] = mine[...]

    tall = n * ROWS
    row = lax.broadcasted_iota(jnp.int32, (tall, n), 0)
    group = lax.broadcasted_iota(jnp.int32, (tall, n), 1)
    spread = jnp.where(group == row // ROWS, 1.0, 0.0).astype(jnp.bfloat16)
    loads[2].wait()
    hits = []
    for t in range(STEPS):
        chosen = sel_ref[t]
        for k in range(2):
            hits.append(jnp.max(jnp.where(chosen == c * 2 + k, 1.0, 0.0), axis=0))
    table = jnp.concatenate(hits, axis=0).astype(jnp.bfloat16)
    marks = lax.dot_general(spread, table, LAST, preferred_element_type=jnp.float32)
    lane = lax.broadcasted_iota(jnp.int32, (tall, STEPS * 4), 1)
    step = lax.broadcasted_iota(jnp.int32, (tall, STEPS * 4), 0) % ROWS // LOCAL_HEADS
    marks = jnp.where(lane // 4 == step, marks, 0.0).astype(jnp.bfloat16)
    source = lax.broadcasted_iota(jnp.int32, (STEPS * 4, 128), 0) % 4
    target = lax.broadcasted_iota(jnp.int32, (STEPS * 4, 128), 1)
    for r in range(2):
        pick = jnp.where((target < 2) & (source == target * 2 + r), 1.0, 0.0).astype(jnp.bfloat16)
        kept = lax.dot_general(marks, pick, FIRST, preferred_element_type=jnp.float32)
        keep[r] = kept.reshape(n, ROWS, 128)

    def x_copy(d, k):
        slot = q_all.at[own, k]
        return remote(slot, slot, x_send.at[d - 1, k], x_recv.at[d - 1, k], at_x(d))

    @pl.loop(0, n)
    def _(k):

        @pl.when((k != z) | other)
        def _():
            q_wait(k)

        for d in (1, 3, 2):
            x_copy(d, k).start()

    for load in loads[3:8]:
        load.wait()

    def px_copy(d, half):
        target = column((x - d + NX) % NX, core)
        return remote(
            part.at[half, target[0] * 2 + target[1]], part_in.at[half, d - 1],
            px_send.at[d - 1, half], px_recv.at[d - 1, half], at_x(-d),
        )

    rows = 2 * far * ROWS
    lane = lax.broadcasted_iota(jnp.int32, (ROWS, 128), 1)

    @pl.loop(0, 4)
    def _(turn):
        half = turn // 2
        r = (request + 1 + turn) % 2
        request_x = 2 * core + r
        away = [(x - request_x - k * (NX - 1 - 2 * request_x) + 2 * NX) % NX for k in range(2)]
        for d in away:
            @pl.when(d > 0)
            def _():
                @pl.loop(half * far, half * far + far)
                def _(k):
                    x_copy(d, k).wait_recv()

        span = pl.ds(half * far, far)
        query = q_all[pl.ds(r * 2, 2), span].reshape(rows, WIDE)
        scores = lax.dot_general(query[:, :KL], lat[r], LAST, preferred_element_type=jnp.float32)
        scores = scores + lax.dot_general(
            query[:, KL:KL + KR], rope[r], FIRST, preferred_element_type=jnp.float32
        )
        scores = scores * SCALE
        length = length_ref[r]
        hits = keep[r, span].reshape(rows // 2, 128)
        hits = jnp.concatenate([hits, hits], axis=0)
        place = lax.broadcasted_iota(jnp.int32, (rows, BLOCK), 1)
        masks, masked = [], []
        for k in range(2):
            mask = (hits[:, k:k + 1] > 0.5) & (place + (c * 2 + k) * BLOCK < length)
            masks.append(mask)
            masked.append(jnp.where(mask, scores[:, k * BLOCK:(k + 1) * BLOCK], NEG))
        top = jnp.maximum(
            jnp.max(masked[0], axis=1, keepdims=True), jnp.max(masked[1], axis=1, keepdims=True)
        )
        top = top.astype(jnp.bfloat16).astype(jnp.float32)
        weights = [jnp.where(m, jnp.exp(v - top), 0.0) for m, v in zip(masks, masked)]
        total = jnp.sum(weights[0], axis=1, keepdims=True) + jnp.sum(weights[1], axis=1, keepdims=True)
        rounded = jnp.concatenate([v.astype(jnp.bfloat16) for v in weights], axis=1)
        out = lax.dot_general(rounded, lat[r], FIRST, preferred_element_type=jnp.float32)
        out = out.astype(jnp.bfloat16)
        high = total.astype(jnp.bfloat16).astype(jnp.float32)
        low = total - high
        for k in range(2):
            stats = jnp.zeros((ROWS, 128), jnp.float32)
            for j in range(far):
                at = slice((k * far + j) * ROWS, (k * far + j + 1) * ROWS)
                part[half, r * 2 + k, :, j * KL:(j + 1) * KL] = out[at]
                for m, term in enumerate((top, high, low)):
                    stats = jnp.where(lane == 3 * j + m, term[at], stats)
            part[half, r * 2 + k, :, far * KL:] = stats.astype(jnp.bfloat16)
        for d in away:
            @pl.when(d > 0)
            def _():
                px_copy(d, half).start()

    mine_k = (y + far) % n
    q_own = q_all[own, mine_k].astype(jnp.float32)
    row_step = lax.broadcasted_iota(jnp.int32, (ROWS, 1), 0) // LOCAL_HEADS
    second = request.astype(jnp.float32)
    new_rows, new_scores = [], []
    for u in range(STEPS):
        both = nl_ref[u].astype(jnp.float32)
        both_rope = nr_ref[u].astype(jnp.float32)
        new_row = both[0:1] * (1.0 - second) + both[1:2] * second
        new_rope = both_rope[0:1] * (1.0 - second) + both_rope[1:2] * second
        score = jnp.sum(q_own[:, :KL] * new_row, axis=1, keepdims=True)
        score = (score + jnp.sum(q_own[:, KL:KL + KR] * new_rope, axis=1, keepdims=True)) * SCALE
        new_rows.append(new_row)
        new_scores.append(jnp.where(row_step >= u, score, NEG))
    new_top = new_scores[0]
    for score in new_scores[1:]:
        new_top = jnp.maximum(new_top, score)

    def py_copy(k):
        to = (k + far) % n
        return remote(joint.at[k], joint_in.at[y], py_send.at[k], py_recv.at[y], (b, to * NX + x))

    @pl.loop(0, 2)
    def _(half):
        for d in (1, 3, 2):
            px_copy(d, half).wait_recv()
        stats = [part[half, own, :, far * KL:].astype(jnp.float32)]
        stats += [part_in[half, e, :, far * KL:].astype(jnp.float32) for e in range(NX - 1)]
        for j in range(far):
            at = slice(j * KL, (j + 1) * KL)
            values = [part[half, own, :, at]] + [part_in[half, e, :, at] for e in range(NX - 1)]
            three = [stat[:, 3 * j:3 * j + 3] for stat in stats]
            k = half * far + j
            joint[k] = packed(*joined(values, three, None))

            @pl.when(k != mine_k)
            def _():
                py_copy(k).start()

    joint_in[y] = joint[mine_k]

    @pl.loop(1, n)
    def _(d):
        k = (y + d) % n
        remote(joint.at[0], joint_in.at[k], py_send.at[0], py_recv.at[k], at_y(d)).wait_recv()

    out, top, total = merged([joint_in[k] for k in range(n)], new_top)
    for u in range(STEPS):
        weight = jnp.where(row_step >= u, jnp.exp(new_scores[u] - top), 0.0)
        total = total + weight
        out = out + weight.astype(jnp.bfloat16).astype(jnp.float32) * new_rows[u]
    done[...] = out / total

    back = remote(done, done_in, back_sem.at[0], back_sem.at[1], origin((mine_k - z + n) % n))
    back.start()
    loads[8].wait()
    back.wait_recv()
    value = done_in[...]

    high = value.astype(jnp.bfloat16)
    rest = value - high.astype(jnp.float32)
    middle = rest.astype(jnp.bfloat16)
    low = (rest - middle.astype(jnp.float32)).astype(jnp.bfloat16)
    terms = jnp.concatenate([high, middle, low], axis=0)
    row_head = lax.broadcasted_iota(jnp.int32, (ROWS, VH), 0) % LOCAL_HEADS
    result = jnp.zeros((ROWS, VH), jnp.float32)
    for h in range(LOCAL_HEADS):
        product = lax.dot_general(terms, w[h], FIRST, preferred_element_type=jnp.float32)
        product = product[:ROWS] + (product[ROWS:2 * ROWS] + product[2 * ROWS:])
        result = jnp.where(row_head == h, product, result)
    gathered[x, y] = result.astype(jnp.bfloat16)

    def oy_copy(d):
        slot = gathered.at[x, y]
        return remote(slot, slot, oy_send.at[d - 1], oy_recv.at[d - 1], at_y(d))

    def ox_copy(d):
        slot = gathered.at[x]
        return remote(slot, slot, ox_send.at[d - 1], ox_recv.at[d - 1], at_x(d))

    @pl.loop(1, n)
    def _(s):
        oy_copy(nearest(n - s)).start()

    @pl.loop(1, n)
    def _(d):
        oy_copy(d).wait_recv()

    for d in (2, 1, 3):
        ox_copy(d).start()
    for d in (1, 3, 2):
        ox_copy(d).wait_recv()
    out_ref[...] = gathered[...]

    back.wait_send()

    @pl.loop(1, n)
    def _(d):
        q_copy(d).wait_send()
        py_copy((mine_k + d) % n).wait_send()
        oy_copy(d).wait_send()

    @pl.when(other)
    def _():
        q_copy(0).wait_send()

    @pl.loop(1, NX)
    def _(d):
        px_copy(d, 0).wait_send()
        px_copy(d, 1).wait_send()
        ox_copy(d).wait_send()

        @pl.loop(0, n)
        def _(k):
            x_copy(d, k).wait_send()


def local(
    q_latent, q_rope, cache_latent, cache_rope, new_latent, new_rope, lengths, selected, w_uv
):
    n = lax.axis_size("ctx") // NX
    selected = jnp.transpose(selected, (0, 3, 1, 2))
    cache_rope = jnp.swapaxes(cache_rope, 1, 2)
    held = cache_latent.shape[1]
    bf16, f32 = jnp.bfloat16, jnp.float32
    dma = pltpu.SemaphoreType.DMA
    anywhere = pl.BlockSpec(memory_space=pl.ANY)
    out = pl.pallas_call(
        functools.partial(kernel, n),
        out_shape=jax.ShapeDtypeStruct((NX, n, ROWS, VH), bf16),
        in_specs=[anywhere] * 9,
        out_specs=pl.BlockSpec(memory_space=pltpu.VMEM),
        scratch_shapes=[
            pltpu.SMEM((2,), jnp.int32),
            pltpu.VMEM(q_latent.shape, bf16),
            pltpu.VMEM(q_rope.shape, bf16),
            pltpu.VMEM(selected.shape, jnp.int32),
            pltpu.VMEM(new_latent.shape, bf16),
            pltpu.VMEM(new_rope.shape, bf16),
            pltpu.VMEM((2, held, KL), bf16),
            pltpu.VMEM((2, KR, held), bf16),
            pltpu.VMEM((LOCAL_HEADS, KL, VH), bf16),
            pltpu.VMEM((ROWS, WIDE), f32),
            pltpu.VMEM((ROWS, WIDE), bf16),
            pltpu.VMEM((NX, n, ROWS, WIDE), bf16),
            pltpu.VMEM((2, n, ROWS, 128), f32),
            pltpu.VMEM((2, NX, ROWS, n // 2 * KL + 128), bf16),
            pltpu.VMEM((2, NX - 1, ROWS, n // 2 * KL + 128), bf16),
            pltpu.VMEM((n, ROWS, WIDE), bf16),
            pltpu.VMEM((n, ROWS, WIDE), bf16),
            pltpu.VMEM((ROWS, KL), f32),
            pltpu.VMEM((ROWS, KL), f32),
            pltpu.VMEM((NX, n, ROWS, VH), bf16),
            dma((9,)),
            dma((n,)), dma((n,)),
            dma((NX - 1, n)), dma((NX - 1, n)),
            dma((NX - 1, 2)), dma((NX - 1, 2)),
            dma((n,)), dma((n,)),
            dma((2,)),
            dma((n - 1,)), dma((n - 1,)),
            dma((NX - 1,)), dma((NX - 1,)),
        ],
        compiler_params=pltpu.CompilerParams(
            collective_id=0, has_side_effects=True, vmem_limit_bytes=60 * 1024 * 1024
        ),
    )(lengths, q_latent, q_rope, selected, new_latent, new_rope, cache_latent, cache_rope, w_uv)
    out = out.reshape(NX, n, STEPS, LOCAL_HEADS, VH)
    return jnp.transpose(out, (2, 1, 0, 3, 4)).reshape(STEPS, NX * n, LOCAL_HEADS, VH)


def solution(mesh):
    placed = (
        P(None, "ctx", "batch", None),
        P(None, "ctx", "batch", None),
        P("batch", "ctx", None),
        P("batch", "ctx", None),
        P(None, "batch", None),
        P(None, "batch", None),
        P("batch"),
        P(None, "batch", None, None),
        P("batch", None, None),
    )
    return jax.shard_map(
        local, mesh=mesh, in_specs=placed, out_specs=P(None, None, "batch", None), check_vma=False
    )
```

```python
import functools

import jax
import jax.numpy as jnp
from jax import lax
from jax.experimental import pallas as pl
from jax.experimental.pallas import tpu as pltpu
from jax.sharding import PartitionSpec as P

MESH = pl.DeviceIdType.MESH
KL = 512
KR = 64
VH = 128
BLOCK = 512
STEPS = 4
NX = 4
LOCAL_HEADS = 4
ROWS = STEPS * LOCAL_HEADS
WIDE = KL + 128
SCALE = (VH + KR) ** (-0.5)
NEG = -1e30
LAST = (((1,), (1,)), ((), ()))
FIRST = (((1,), (0,)), ((), ()))


def column(x, core):
    source_core = (x // 2 + core) % 2
    source_x = x + source_core * (NX - 1 - 2 * x)
    request = source_x % 2
    return request, source_core, source_x


def packed(out, top, total):
    lane = lax.broadcasted_iota(jnp.int32, (out.shape[0], 128), 1)
    high = total.astype(jnp.bfloat16).astype(jnp.float32)
    stats = jnp.where(lane == 0, top, jnp.where(lane == 1, high, jnp.where(lane == 2, total - high, 0.0)))
    return jnp.concatenate([out.astype(jnp.bfloat16), stats.astype(jnp.bfloat16)], axis=1)


def merged(parts, top):
    stats = [part[:, KL:].astype(jnp.float32)[:, :3] for part in parts]
    return joined([part[:, :KL] for part in parts], stats, top)


def joined(values, stats, top):
    for stat in stats:
        top = stat[:, 0:1] if top is None else jnp.maximum(top, stat[:, 0:1])
    out, total = None, None
    for value, stat in zip(values, stats):
        factor = jnp.exp(stat[:, 0:1] - top)
        share = factor * (stat[:, 1:2] + stat[:, 2:3])
        term = factor * value.astype(jnp.float32)
        out = term if out is None else out + term
        total = share if total is None else total + share
    return out, top, total


def kernel(
    n,
    length_hbm, ql_hbm, qr_hbm, sel_hbm, nl_hbm, nr_hbm, lat_hbm, rope_hbm, w_hbm,
    out_ref,
    length_ref, ql_ref, qr_ref, sel_ref, nl_ref, nr_ref, lat, rope, w, rows32, mine, q_all, keep,
    part, part_in, joint, joint_in, done, done_in, gathered,
    local_sem, q_send, q_recv, x_send, x_recv, px_send, px_recv, py_send, py_recv, back_sem,
    oy_send, oy_recv, ox_send, ox_recv,
):
    b, c = lax.axis_index("batch"), lax.axis_index("ctx")
    z, core = b // 2, b % 2
    y, x = c // NX, c % NX
    far = n // 2
    few = max(1, n // 4)
    groups = n // few

    pairs = (
        (ql_hbm, ql_ref), (qr_hbm, qr_ref), (sel_hbm, sel_ref), (nl_hbm, nl_ref), (nr_hbm, nr_ref),
        (length_hbm, length_ref), (lat_hbm, lat), (rope_hbm, rope), (w_hbm, w),
    )
    loads = [pltpu.make_async_copy(src, dst, local_sem.at[k]) for k, (src, dst) in enumerate(pairs)]
    for load in loads:
        load.start()

    def at_y(step):
        return (b, ((y + step + n) % n) * NX + x)

    def at_x(step):
        return (b, y * NX + (x + step + NX) % NX)

    request, source_core, source_x = column(x, core)
    own = request * 2 + source_core
    goal_x = x + core * (NX - 1 - 2 * x)
    goal_column = (x % 2) * 2 + core
    itself = (y == z) & (x // 2 == core) & (goal_x == x)
    other = jnp.logical_not(itself)

    def goal(step):
        return (y * 2 + x // 2, ((y + step) % n) * NX + goal_x)

    def origin(step):
        return (((z + step) % n) * 2 + source_core, z * NX + source_x)

    barrier = pltpu.get_barrier_semaphore()

    def greet(device):
        pl.semaphore_signal(barrier, inc=1, device_id=device, device_id_type=MESH)

    @pl.loop(1, n)
    def _(d):
        greet(goal(d))
        greet(origin(d))
        greet(at_y(d))

    @pl.loop(1, NX)
    def _(d):
        greet(at_x(d))

    @pl.when(other)
    def _():
        greet(goal(0))
        greet(origin(0))

    loads[0].wait()
    loads[1].wait()
    for t in range(STEPS):
        span = pl.ds(t * LOCAL_HEADS, LOCAL_HEADS)
        rows32[span, :KL] = ql_ref[t, 0].astype(jnp.float32)
        rows32[span, KL:KL + KR] = qr_ref[t, 0].astype(jnp.float32)
    rows32[:, KL + KR:] = jnp.zeros((ROWS, WIDE - KL - KR), jnp.float32)
    mine[...] = rows32[...].astype(jnp.bfloat16)

    pl.semaphore_wait(barrier, 3 * (n - 1) + NX - 1 + 2 * other.astype(jnp.int32))

    def remote(src, dst, send, recv, device):
        return pltpu.make_async_remote_copy(
            src_ref=src, dst_ref=dst, send_sem=send, recv_sem=recv, device_id=device, device_id_type=MESH
        )

    def nearest(s):
        return s % 2 * ((s + 1) // 2) + (1 - s % 2) * ((n - s // 2) % n)

    def q_copy(d):
        return remote(mine, q_all.at[goal_column, z], q_send.at[d], q_recv.at[z], goal(d))

    def q_wait(k):
        slot = q_all.at[own, k]
        remote(slot, slot, q_send.at[0], q_recv.at[k], goal(0)).wait_recv()

    @pl.loop(1, n)
    def _(s):
        q_copy(nearest(n - s)).start()

    @pl.when(other)
    def _():
        q_copy(0).start()

    @pl.when(itself)
    def _():
        q_all[own, z] = mine[...]

    tall = n * ROWS
    row = lax.broadcasted_iota(jnp.int32, (tall, n), 0)
    group = lax.broadcasted_iota(jnp.int32, (tall, n), 1)
    spread = jnp.where(group == row // ROWS, 1.0, 0.0).astype(jnp.bfloat16)
    loads[2].wait()
    hits = []
    for t in range(STEPS):
        chosen = sel_ref[t]
        for k in range(2):
            hits.append(jnp.max(jnp.where(chosen == c * 2 + k, 1.0, 0.0), axis=0))
    table = jnp.concatenate(hits, axis=0).astype(jnp.bfloat16)
    marks = lax.dot_general(spread, table, LAST, preferred_element_type=jnp.float32)
    lane = lax.broadcasted_iota(jnp.int32, (tall, STEPS * 4), 1)
    step = lax.broadcasted_iota(jnp.int32, (tall, STEPS * 4), 0) % ROWS // LOCAL_HEADS
    marks = jnp.where(lane // 4 == step, marks, 0.0).astype(jnp.bfloat16)
    source = lax.broadcasted_iota(jnp.int32, (STEPS * 4, 128), 0) % 4
    target = lax.broadcasted_iota(jnp.int32, (STEPS * 4, 128), 1)
    for r in range(2):
        pick = jnp.where((target < 2) & (source == target * 2 + r), 1.0, 0.0).astype(jnp.bfloat16)
        kept = lax.dot_general(marks, pick, FIRST, preferred_element_type=jnp.float32)
        keep[r] = kept.reshape(n, ROWS, 128)

    def x_copy(d, k):
        slot = q_all.at[own, k]
        return remote(slot, slot, x_send.at[d - 1, k], x_recv.at[d - 1, k], at_x(d))

    @pl.loop(0, n)
    def _(k):

        @pl.when((k != z) | other)
        def _():
            q_wait(k)

        for d in (1, 3, 2):
            x_copy(d, k).start()

    for load in loads[3:8]:
        load.wait()

    def px_copy(d, half):
        target = column((x - d + NX) % NX, core)
        return remote(
            part.at[half, target[0] * 2 + target[1]], part_in.at[half, d - 1],
            px_send.at[d - 1, half], px_recv.at[d - 1, half], at_x(-d),
        )

    rows = 2 * few * ROWS
    lane = lax.broadcasted_iota(jnp.int32, (ROWS, 128), 1)

    @pl.loop(0, 2 * groups)
    def _(turn):
        half = turn // 2
        r = (request + 1 + turn) % 2
        request_x = 2 * core + r
        away = [(x - request_x - k * (NX - 1 - 2 * request_x) + 2 * NX) % NX for k in range(2)]
        for d in away:
            @pl.when(d > 0)
            def _():
                @pl.loop(half * few, half * few + few)
                def _(k):
                    x_copy(d, k).wait_recv()

        span = pl.ds(half * few, few)
        query = q_all[pl.ds(r * 2, 2), span].reshape(rows, WIDE)
        scores = lax.dot_general(query[:, :KL], lat[r], LAST, preferred_element_type=jnp.float32)
        scores = scores + lax.dot_general(
            query[:, KL:KL + KR], rope[r], FIRST, preferred_element_type=jnp.float32
        )
        scores = scores * SCALE
        length = length_ref[r]
        hits = keep[r, span].reshape(rows // 2, 128)
        hits = jnp.concatenate([hits, hits], axis=0)
        place = lax.broadcasted_iota(jnp.int32, (rows, BLOCK), 1)
        masks, masked = [], []
        for k in range(2):
            mask = (hits[:, k:k + 1] > 0.5) & (place + (c * 2 + k) * BLOCK < length)
            masks.append(mask)
            masked.append(jnp.where(mask, scores[:, k * BLOCK:(k + 1) * BLOCK], NEG))
        top = jnp.maximum(
            jnp.max(masked[0], axis=1, keepdims=True), jnp.max(masked[1], axis=1, keepdims=True)
        )
        top = top.astype(jnp.bfloat16).astype(jnp.float32)
        weights = [jnp.where(m, jnp.exp(v - top), 0.0) for m, v in zip(masks, masked)]
        total = jnp.sum(weights[0], axis=1, keepdims=True) + jnp.sum(weights[1], axis=1, keepdims=True)
        rounded = jnp.concatenate([v.astype(jnp.bfloat16) for v in weights], axis=1)
        out = lax.dot_general(rounded, lat[r], FIRST, preferred_element_type=jnp.float32)
        out = out.astype(jnp.bfloat16)
        high = total.astype(jnp.bfloat16).astype(jnp.float32)
        low = total - high
        for k in range(2):
            stats = jnp.zeros((ROWS, 128), jnp.float32)
            for j in range(few):
                at = slice((k * few + j) * ROWS, (k * few + j + 1) * ROWS)
                part[half, r * 2 + k, :, j * KL:(j + 1) * KL] = out[at]
                for m, term in enumerate((top, high, low)):
                    stats = jnp.where(lane == 3 * j + m, term[at], stats)
            part[half, r * 2 + k, :, few * KL:] = stats.astype(jnp.bfloat16)
        for d in away:
            @pl.when(d > 0)
            def _():
                px_copy(d, half).start()

    mine_k = (y + far) % n
    q_own = q_all[own, mine_k].astype(jnp.float32)
    row_step = lax.broadcasted_iota(jnp.int32, (ROWS, 1), 0) // LOCAL_HEADS
    second = request.astype(jnp.float32)
    new_rows, new_scores = [], []
    for u in range(STEPS):
        both = nl_ref[u].astype(jnp.float32)
        both_rope = nr_ref[u].astype(jnp.float32)
        new_row = both[0:1] * (1.0 - second) + both[1:2] * second
        new_rope = both_rope[0:1] * (1.0 - second) + both_rope[1:2] * second
        score = jnp.sum(q_own[:, :KL] * new_row, axis=1, keepdims=True)
        score = (score + jnp.sum(q_own[:, KL:KL + KR] * new_rope, axis=1, keepdims=True)) * SCALE
        new_rows.append(new_row)
        new_scores.append(jnp.where(row_step >= u, score, NEG))
    new_top = new_scores[0]
    for score in new_scores[1:]:
        new_top = jnp.maximum(new_top, score)

    def py_copy(k):
        to = (k + far) % n
        return remote(joint.at[k], joint_in.at[y], py_send.at[k], py_recv.at[y], (b, to * NX + x))

    @pl.loop(0, groups)
    def _(half):
        for d in (1, 3, 2):
            px_copy(d, half).wait_recv()
        stats = [part[half, own, :, few * KL:].astype(jnp.float32)]
        stats += [part_in[half, e, :, few * KL:].astype(jnp.float32) for e in range(NX - 1)]
        for j in range(few):
            at = slice(j * KL, (j + 1) * KL)
            values = [part[half, own, :, at]] + [part_in[half, e, :, at] for e in range(NX - 1)]
            three = [stat[:, 3 * j:3 * j + 3] for stat in stats]
            k = half * few + j
            joint[k] = packed(*joined(values, three, None))

            @pl.when(k != mine_k)
            def _():
                py_copy(k).start()

    joint_in[y] = joint[mine_k]

    @pl.loop(1, n)
    def _(d):
        k = (y + d) % n
        remote(joint.at[0], joint_in.at[k], py_send.at[0], py_recv.at[k], at_y(d)).wait_recv()

    out, top, total = merged([joint_in[k] for k in range(n)], new_top)
    for u in range(STEPS):
        weight = jnp.where(row_step >= u, jnp.exp(new_scores[u] - top), 0.0)
        total = total + weight
        out = out + weight.astype(jnp.bfloat16).astype(jnp.float32) * new_rows[u]
    done[...] = out / total

    back = remote(done, done_in, back_sem.at[0], back_sem.at[1], origin((mine_k - z + n) % n))
    back.start()
    loads[8].wait()
    back.wait_recv()
    value = done_in[...]

    high = value.astype(jnp.bfloat16)
    rest = value - high.astype(jnp.float32)
    middle = rest.astype(jnp.bfloat16)
    low = (rest - middle.astype(jnp.float32)).astype(jnp.bfloat16)
    terms = jnp.concatenate([high, middle, low], axis=0)
    row_head = lax.broadcasted_iota(jnp.int32, (ROWS, VH), 0) % LOCAL_HEADS
    result = jnp.zeros((ROWS, VH), jnp.float32)
    for h in range(LOCAL_HEADS):
        product = lax.dot_general(terms, w[h], FIRST, preferred_element_type=jnp.float32)
        product = product[:ROWS] + (product[ROWS:2 * ROWS] + product[2 * ROWS:])
        result = jnp.where(row_head == h, product, result)
    gathered[x, y] = result.astype(jnp.bfloat16)

    def oy_copy(d):
        slot = gathered.at[x, y]
        return remote(slot, slot, oy_send.at[d - 1], oy_recv.at[d - 1], at_y(d))

    def ox_copy(d):
        return remote(gathered.at[x], out_ref.at[x], ox_send.at[d - 1], ox_recv.at[d - 1], at_x(d))

    @pl.loop(1, n)
    def _(s):
        oy_copy(nearest(n - s)).start()

    @pl.loop(1, n)
    def _(d):
        oy_copy(d).wait_recv()

    for d in (2, 1, 3):
        ox_copy(d).start()
    keep_own = pltpu.make_async_copy(gathered.at[x], out_ref.at[x], local_sem.at[9])
    keep_own.start()
    for d in (1, 3, 2):
        ox_copy(d).wait_recv()
    keep_own.wait()

    back.wait_send()

    @pl.loop(1, n)
    def _(d):
        q_copy(d).wait_send()
        py_copy((mine_k + d) % n).wait_send()
        oy_copy(d).wait_send()

    @pl.when(other)
    def _():
        q_copy(0).wait_send()

    @pl.loop(1, NX)
    def _(d):
        for half in range(groups):
            px_copy(d, half).wait_send()
        ox_copy(d).wait_send()

        @pl.loop(0, n)
        def _(k):
            x_copy(d, k).wait_send()


def local(
    q_latent, q_rope, cache_latent, cache_rope, new_latent, new_rope, lengths, selected, w_uv
):
    n = lax.axis_size("ctx") // NX
    selected = jnp.transpose(selected, (0, 3, 1, 2))
    cache_rope = jnp.swapaxes(cache_rope, 1, 2)
    held = cache_latent.shape[1]
    few = max(1, n // 4)
    bf16, f32 = jnp.bfloat16, jnp.float32
    dma = pltpu.SemaphoreType.DMA
    anywhere = pl.BlockSpec(memory_space=pl.ANY)
    out = pl.pallas_call(
        functools.partial(kernel, n),
        out_shape=jax.ShapeDtypeStruct((NX, n, ROWS, VH), bf16),
        in_specs=[anywhere] * 9,
        out_specs=anywhere,
        scratch_shapes=[
            pltpu.SMEM((2,), jnp.int32),
            pltpu.VMEM(q_latent.shape, bf16),
            pltpu.VMEM(q_rope.shape, bf16),
            pltpu.VMEM(selected.shape, jnp.int32),
            pltpu.VMEM(new_latent.shape, bf16),
            pltpu.VMEM(new_rope.shape, bf16),
            pltpu.VMEM((2, held, KL), bf16),
            pltpu.VMEM((2, KR, held), bf16),
            pltpu.VMEM((LOCAL_HEADS, KL, VH), bf16),
            pltpu.VMEM((ROWS, WIDE), f32),
            pltpu.VMEM((ROWS, WIDE), bf16),
            pltpu.VMEM((NX, n, ROWS, WIDE), bf16),
            pltpu.VMEM((2, n, ROWS, 128), f32),
            pltpu.VMEM((n // few, NX, ROWS, few * KL + 128), bf16),
            pltpu.VMEM((n // few, NX - 1, ROWS, few * KL + 128), bf16),
            pltpu.VMEM((n, ROWS, WIDE), bf16),
            pltpu.VMEM((n, ROWS, WIDE), bf16),
            pltpu.VMEM((ROWS, KL), f32),
            pltpu.VMEM((ROWS, KL), f32),
            pltpu.VMEM((NX, n, ROWS, VH), bf16),
            dma((10,)),
            dma((n,)), dma((n,)),
            dma((NX - 1, n)), dma((NX - 1, n)),
            dma((NX - 1, n // few)), dma((NX - 1, n // few)),
            dma((n,)), dma((n,)),
            dma((2,)),
            dma((n - 1,)), dma((n - 1,)),
            dma((NX - 1,)), dma((NX - 1,)),
        ],
        compiler_params=pltpu.CompilerParams(
            collective_id=0, has_side_effects=True, vmem_limit_bytes=60 * 1024 * 1024
        ),
    )(lengths, q_latent, q_rope, selected, new_latent, new_rope, cache_latent, cache_rope, w_uv)
    out = out.reshape(NX, n, STEPS, LOCAL_HEADS, VH)
    return jnp.transpose(out, (2, 1, 0, 3, 4)).reshape(STEPS, NX * n, LOCAL_HEADS, VH)


def solution(mesh):
    placed = (
        P(None, "ctx", "batch", None),
        P(None, "ctx", "batch", None),
        P("batch", "ctx", None),
        P("batch", "ctx", None),
        P(None, "batch", None),
        P(None, "batch", None),
        P("batch"),
        P(None, "batch", None, None),
        P("batch", None, None),
    )
    return jax.shard_map(
        local, mesh=mesh, in_specs=placed, out_specs=P(None, None, "batch", None), check_vma=False
    )
```

```python
import functools

import jax
import jax.numpy as jnp
from jax import lax
from jax.experimental import pallas as pl
from jax.experimental.pallas import tpu as pltpu
from jax.sharding import PartitionSpec as P

MESH = pl.DeviceIdType.MESH
KL = 512
KR = 64
VH = 128
BLOCK = 512
STEPS = 4
NX = 4
LOCAL_HEADS = 4
ROWS = STEPS * LOCAL_HEADS
WIDE = KL + 128
SCALE = (VH + KR) ** (-0.5)
NEG = -1e30
LAST = (((1,), (1,)), ((), ()))
FIRST = (((1,), (0,)), ((), ()))


def mod(value, size):
    return value % size if isinstance(value, int) else lax.rem(value, size)


def div(value, size):
    return value // size if isinstance(value, int) else lax.div(value, size)


def column(x, core):
    source_core = mod(div(x, 2) + core, 2)
    source_x = x + source_core * (NX - 1 - 2 * x)
    request = mod(source_x, 2)
    return request, source_core, source_x


def packed(out, top, total):
    lane = lax.broadcasted_iota(jnp.int32, (out.shape[0], 128), 1)
    high = total.astype(jnp.bfloat16).astype(jnp.float32)
    stats = jnp.where(lane == 0, top, jnp.where(lane == 1, high, jnp.where(lane == 2, total - high, 0.0)))
    return jnp.concatenate([out.astype(jnp.bfloat16), stats.astype(jnp.bfloat16)], axis=1)


def merged(parts, top):
    stats = [part[:, KL:].astype(jnp.float32)[:, :3] for part in parts]
    return joined([part[:, :KL] for part in parts], stats, top)


def joined(values, stats, top):
    for stat in stats:
        top = stat[:, 0:1] if top is None else jnp.maximum(top, stat[:, 0:1])
    out, total = None, None
    for value, stat in zip(values, stats):
        factor = jnp.exp(stat[:, 0:1] - top)
        share = factor * (stat[:, 1:2] + stat[:, 2:3])
        term = factor * value.astype(jnp.float32)
        out = term if out is None else out + term
        total = share if total is None else total + share
    return out, top, total


def kernel(
    n,
    length_hbm, ql_hbm, qr_hbm, sel_hbm, nl_hbm, nr_hbm, lat_hbm, rope_hbm, w_hbm,
    out_ref,
    length_ref, ql_ref, qr_ref, sel_ref, nl_ref, nr_ref, lat, rope, w, rows32, mine, q_all, keep,
    part, part_in, joint, joint_in, done, done_in, final,
    local_sem, q_send, q_recv, x_send, x_recv, px_send, px_recv, py_send, py_recv, back_sem,
    o_send, o_recv,
):
    b, c = lax.axis_index("batch"), lax.axis_index("ctx")
    z, core = div(b, 2), mod(b, 2)
    y, x = div(c, NX), mod(c, NX)
    far = n // 2
    few = max(1, n // 4)
    groups = n // few

    pairs = (
        (ql_hbm, ql_ref), (qr_hbm, qr_ref), (sel_hbm, sel_ref), (nl_hbm, nl_ref), (nr_hbm, nr_ref),
        (length_hbm, length_ref), (lat_hbm, lat), (rope_hbm, rope), (w_hbm, w),
    )
    loads = [pltpu.make_async_copy(src, dst, local_sem.at[k]) for k, (src, dst) in enumerate(pairs)]
    for load in loads:
        load.start()

    def at_y(step):
        return (b, mod(y + step, n) * NX + x)

    def at_x(step):
        return (b, y * NX + mod(x + step + NX, NX))

    request, source_core, source_x = column(x, core)
    own = request * 2 + source_core
    goal_x = x + core * (NX - 1 - 2 * x)
    goal_column = mod(x, 2) * 2 + core
    itself = (y == z) & (div(x, 2) == core) & (goal_x == x)
    other = jnp.logical_not(itself)

    def goal(step):
        return (y * 2 + div(x, 2), mod(y + step, n) * NX + goal_x)

    def origin(step):
        return (mod(z + step, n) * 2 + source_core, z * NX + source_x)

    barrier = pltpu.get_barrier_semaphore()

    def greet(device):
        pl.semaphore_signal(barrier, inc=1, device_id=device, device_id_type=MESH)

    for d in range(1, n):
        greet(goal(d))
        greet(origin(d))
        greet(at_y(d))
    for d in range(1, NX):
        greet(at_x(d))

    @pl.when(other)
    def _():
        greet(goal(0))
        greet(origin(0))

    loads[0].wait()
    loads[1].wait()
    for t in range(STEPS):
        span = pl.ds(t * LOCAL_HEADS, LOCAL_HEADS)
        rows32[span, :KL] = ql_ref[t, 0].astype(jnp.float32)
        rows32[span, KL:KL + KR] = qr_ref[t, 0].astype(jnp.float32)
    rows32[:, KL + KR:] = jnp.zeros((ROWS, WIDE - KL - KR), jnp.float32)
    mine[...] = rows32[...].astype(jnp.bfloat16)

    pl.semaphore_wait(barrier, 3 * (n - 1) + NX - 1 + 2 * other.astype(jnp.int32))

    def remote(src, dst, send, recv, device):
        return pltpu.make_async_remote_copy(
            src_ref=src, dst_ref=dst, send_sem=send, recv_sem=recv, device_id=device, device_id_type=MESH
        )

    def nearest(s):
        return mod(s, 2) * div(s + 1, 2) + (1 - mod(s, 2)) * mod(n - div(s, 2), n)

    def q_copy(d):
        return remote(mine, q_all.at[goal_column, z], q_send.at[d], q_recv.at[z], goal(d))

    def q_wait(k):
        slot = q_all.at[own, k]
        remote(slot, slot, q_send.at[0], q_recv.at[k], goal(0)).wait_recv()

    for s in range(1, n):
        q_copy(nearest(n - s)).start()

    @pl.when(other)
    def _():
        q_copy(0).start()

    @pl.when(itself)
    def _():
        q_all[own, z] = mine[...]

    tall = n * ROWS
    row = lax.broadcasted_iota(jnp.int32, (tall, n), 0)
    group = lax.broadcasted_iota(jnp.int32, (tall, n), 1)
    spread = jnp.where(group == row // ROWS, 1.0, 0.0).astype(jnp.bfloat16)
    loads[2].wait()
    hits = []
    for t in range(STEPS):
        chosen = sel_ref[t]
        for k in range(2):
            hits.append(jnp.max(jnp.where(chosen == c * 2 + k, 1.0, 0.0), axis=0))
    table = jnp.concatenate(hits, axis=0).astype(jnp.bfloat16)
    marks = lax.dot_general(spread, table, LAST, preferred_element_type=jnp.float32)
    lane = lax.broadcasted_iota(jnp.int32, (tall, STEPS * 4), 1)
    step = lax.broadcasted_iota(jnp.int32, (tall, STEPS * 4), 0) % ROWS // LOCAL_HEADS
    marks = jnp.where(lane // 4 == step, marks, 0.0).astype(jnp.bfloat16)
    source = lax.broadcasted_iota(jnp.int32, (STEPS * 4, 128), 0) % 4
    target = lax.broadcasted_iota(jnp.int32, (STEPS * 4, 128), 1)
    for r in range(2):
        pick = jnp.where((target < 2) & (source == target * 2 + r), 1.0, 0.0).astype(jnp.bfloat16)
        kept = lax.dot_general(marks, pick, FIRST, preferred_element_type=jnp.float32)
        keep[r] = kept.reshape(n, ROWS, 128)

    def x_copy(d, k):
        slot = q_all.at[own, k]
        return remote(slot, slot, x_send.at[d - 1, k], x_recv.at[d - 1, k], at_x(d))

    @pl.loop(0, n)
    def _(k):

        @pl.when((k != z) | other)
        def _():
            q_wait(k)

        for d in (1, 3, 2):
            x_copy(d, k).start()

    for load in loads[3:8]:
        load.wait()

    def px_copy(d, half):
        target = column(mod(x - d + NX, NX), core)
        return remote(
            part.at[half, target[0] * 2 + target[1]], part_in.at[half, d - 1],
            px_send.at[d - 1, half], px_recv.at[d - 1, half], at_x(-d),
        )

    rows = 2 * few * ROWS
    lane = lax.broadcasted_iota(jnp.int32, (ROWS, 128), 1)

    @pl.loop(0, 2 * groups)
    def _(turn):
        half = div(turn, 2)
        r = mod(request + 1 + turn, 2)
        request_x = 2 * core + r
        away = [mod(x - request_x - k * (NX - 1 - 2 * request_x) + 2 * NX, NX) for k in range(2)]
        for d in away:
            @pl.when(d > 0)
            def _():
                @pl.loop(half * few, half * few + few)
                def _(k):
                    x_copy(d, k).wait_recv()

        span = pl.ds(half * few, few)
        query = q_all[pl.ds(r * 2, 2), span].reshape(rows, WIDE)
        scores = lax.dot_general(query[:, :KL], lat[r], LAST, preferred_element_type=jnp.float32)
        scores = scores + lax.dot_general(
            query[:, KL:KL + KR], rope[r], FIRST, preferred_element_type=jnp.float32
        )
        scores = scores * SCALE
        length = length_ref[r]
        hits = keep[r, span].reshape(rows // 2, 128)
        hits = jnp.concatenate([hits, hits], axis=0)
        place = lax.broadcasted_iota(jnp.int32, (rows, BLOCK), 1)
        masks, masked = [], []
        for k in range(2):
            mask = (hits[:, k:k + 1] > 0.5) & (place + (c * 2 + k) * BLOCK < length)
            masks.append(mask)
            masked.append(jnp.where(mask, scores[:, k * BLOCK:(k + 1) * BLOCK], NEG))
        top = jnp.maximum(
            jnp.max(masked[0], axis=1, keepdims=True), jnp.max(masked[1], axis=1, keepdims=True)
        )
        top = top.astype(jnp.bfloat16).astype(jnp.float32)
        weights = [jnp.where(m, jnp.exp(v - top), 0.0) for m, v in zip(masks, masked)]
        total = jnp.sum(weights[0], axis=1, keepdims=True) + jnp.sum(weights[1], axis=1, keepdims=True)
        rounded = jnp.concatenate([v.astype(jnp.bfloat16) for v in weights], axis=1)
        out = lax.dot_general(rounded, lat[r], FIRST, preferred_element_type=jnp.float32)
        out = out.astype(jnp.bfloat16)
        high = total.astype(jnp.bfloat16).astype(jnp.float32)
        low = total - high
        for k in range(2):
            stats = jnp.zeros((ROWS, 128), jnp.float32)
            for j in range(few):
                at = slice((k * few + j) * ROWS, (k * few + j + 1) * ROWS)
                part[half, r * 2 + k, :, j * KL:(j + 1) * KL] = out[at]
                for m, term in enumerate((top, high, low)):
                    stats = jnp.where(lane == 3 * j + m, term[at], stats)
            part[half, r * 2 + k, :, few * KL:] = stats.astype(jnp.bfloat16)
        for d in away:
            @pl.when(d > 0)
            def _():
                px_copy(d, half).start()

    mine_k = mod(y + far, n)
    q_own = q_all[own, mine_k].astype(jnp.float32)
    row_step = lax.broadcasted_iota(jnp.int32, (ROWS, 1), 0) // LOCAL_HEADS
    second = request.astype(jnp.float32)
    new_rows, new_scores = [], []
    for u in range(STEPS):
        both = nl_ref[u].astype(jnp.float32)
        both_rope = nr_ref[u].astype(jnp.float32)
        new_row = both[0:1] * (1.0 - second) + both[1:2] * second
        new_rope = both_rope[0:1] * (1.0 - second) + both_rope[1:2] * second
        score = jnp.sum(q_own[:, :KL] * new_row, axis=1, keepdims=True)
        score = (score + jnp.sum(q_own[:, KL:KL + KR] * new_rope, axis=1, keepdims=True)) * SCALE
        new_rows.append(new_row)
        new_scores.append(jnp.where(row_step >= u, score, NEG))
    new_top = new_scores[0]
    for score in new_scores[1:]:
        new_top = jnp.maximum(new_top, score)

    def py_copy(k):
        to = mod(k + far, n)
        return remote(joint.at[k], joint_in.at[y], py_send.at[k], py_recv.at[y], (b, to * NX + x))

    @pl.loop(0, groups)
    def _(half):
        for d in (1, 3, 2):
            px_copy(d, half).wait_recv()
        stats = [part[half, own, :, few * KL:].astype(jnp.float32)]
        stats += [part_in[half, e, :, few * KL:].astype(jnp.float32) for e in range(NX - 1)]
        for j in range(few):
            at = slice(j * KL, (j + 1) * KL)
            values = [part[half, own, :, at]] + [part_in[half, e, :, at] for e in range(NX - 1)]
            three = [stat[:, 3 * j:3 * j + 3] for stat in stats]
            k = half * few + j
            joint[k] = packed(*joined(values, three, None))

            @pl.when(k != mine_k)
            def _():
                py_copy(k).start()

    joint_in[y] = joint[mine_k]

    @pl.loop(1, n)
    def _(d):
        k = mod(y + d, n)
        remote(joint.at[0], joint_in.at[k], py_send.at[0], py_recv.at[k], at_y(d)).wait_recv()

    out, top, total = merged([joint_in[k] for k in range(n)], new_top)
    for u in range(STEPS):
        weight = jnp.where(row_step >= u, jnp.exp(new_scores[u] - top), 0.0)
        total = total + weight
        out = out + weight.astype(jnp.bfloat16).astype(jnp.float32) * new_rows[u]
    done[...] = out / total

    back = remote(done, done_in, back_sem.at[0], back_sem.at[1], origin(mod(mine_k - z + n, n)))
    back.start()
    loads[8].wait()
    back.wait_recv()
    value = done_in[...]

    high = value.astype(jnp.bfloat16)
    rest = value - high.astype(jnp.float32)
    middle = rest.astype(jnp.bfloat16)
    low = (rest - middle.astype(jnp.float32)).astype(jnp.bfloat16)
    terms = jnp.concatenate([high, middle, low], axis=0)
    row_head = lax.broadcasted_iota(jnp.int32, (ROWS, VH), 0) % LOCAL_HEADS
    result = jnp.zeros((ROWS, VH), jnp.float32)
    for h in range(LOCAL_HEADS):
        product = lax.dot_general(terms, w[h], FIRST, preferred_element_type=jnp.float32)
        product = product[:ROWS] + (product[ROWS:2 * ROWS] + product[2 * ROWS:])
        result = jnp.where(row_head == h, product, result)
    final[...] = result.astype(jnp.bfloat16)

    def o_copy(dy, dx):
        target = (b, mod(y + dy, n) * NX + mod(x + dx, NX))
        return remote(final, out_ref.at[x, y], o_send.at[dx, dy], o_recv.at[dx, dy], target)

    @pl.loop(0, n - 1)
    def _(s):
        dy = nearest(n - 1 - s)
        for dx in (2, 1, 3, 0):
            o_copy(dy, dx).start()

    for dx in (2, 1, 3):
        o_copy(0, dx).start()
    keep_own = pltpu.make_async_copy(final, out_ref.at[x, y], local_sem.at[9])
    keep_own.start()

    @pl.loop(1, n * NX)
    def _(k):
        o_copy(div(k, NX), mod(k, NX)).wait_recv()

    keep_own.wait()

    @pl.loop(1, n * NX)
    def _(k):
        o_copy(div(k, NX), mod(k, NX)).wait_send()

    back.wait_send()

    @pl.loop(1, n)
    def _(d):
        q_copy(d).wait_send()
        py_copy(mod(mine_k + d, n)).wait_send()

    @pl.when(other)
    def _():
        q_copy(0).wait_send()

    @pl.loop(1, NX)
    def _(d):
        for half in range(groups):
            px_copy(d, half).wait_send()

        @pl.loop(0, n)
        def _(k):
            x_copy(d, k).wait_send()


def local(
    q_latent, q_rope, cache_latent, cache_rope, new_latent, new_rope, lengths, selected, w_uv
):
    n = lax.axis_size("ctx") // NX
    selected = jnp.transpose(selected, (0, 3, 1, 2))
    cache_rope = jnp.swapaxes(cache_rope, 1, 2)
    held = cache_latent.shape[1]
    few = max(1, n // 4)
    bf16, f32 = jnp.bfloat16, jnp.float32
    dma = pltpu.SemaphoreType.DMA
    anywhere = pl.BlockSpec(memory_space=pl.ANY)
    out = pl.pallas_call(
        functools.partial(kernel, n),
        out_shape=jax.ShapeDtypeStruct((NX, n, ROWS, VH), bf16),
        in_specs=[anywhere] * 9,
        out_specs=anywhere,
        scratch_shapes=[
            pltpu.SMEM((2,), jnp.int32),
            pltpu.VMEM(q_latent.shape, bf16),
            pltpu.VMEM(q_rope.shape, bf16),
            pltpu.VMEM(selected.shape, jnp.int32),
            pltpu.VMEM(new_latent.shape, bf16),
            pltpu.VMEM(new_rope.shape, bf16),
            pltpu.VMEM((2, held, KL), bf16),
            pltpu.VMEM((2, KR, held), bf16),
            pltpu.VMEM((LOCAL_HEADS, KL, VH), bf16),
            pltpu.VMEM((ROWS, WIDE), f32),
            pltpu.VMEM((ROWS, WIDE), bf16),
            pltpu.VMEM((NX, n, ROWS, WIDE), bf16),
            pltpu.VMEM((2, n, ROWS, 128), f32),
            pltpu.VMEM((n // few, NX, ROWS, few * KL + 128), bf16),
            pltpu.VMEM((n // few, NX - 1, ROWS, few * KL + 128), bf16),
            pltpu.VMEM((n, ROWS, WIDE), bf16),
            pltpu.VMEM((n, ROWS, WIDE), bf16),
            pltpu.VMEM((ROWS, KL), f32),
            pltpu.VMEM((ROWS, KL), f32),
            pltpu.VMEM((ROWS, VH), bf16),
            dma((10,)),
            dma((n,)), dma((n,)),
            dma((NX - 1, n)), dma((NX - 1, n)),
            dma((NX - 1, n // few)), dma((NX - 1, n // few)),
            dma((n,)), dma((n,)),
            dma((2,)),
            dma((NX, n)), dma((NX, n)),
        ],
        compiler_params=pltpu.CompilerParams(
            collective_id=0, has_side_effects=True, vmem_limit_bytes=60 * 1024 * 1024
        ),
    )(lengths, q_latent, q_rope, selected, new_latent, new_rope, cache_latent, cache_rope, w_uv)
    out = out.reshape(NX, n, STEPS, LOCAL_HEADS, VH)
    return jnp.transpose(out, (2, 1, 0, 3, 4)).reshape(STEPS, NX * n, LOCAL_HEADS, VH)


def solution(mesh):
    placed = (
        P(None, "ctx", "batch", None),
        P(None, "ctx", "batch", None),
        P("batch", "ctx", None),
        P("batch", "ctx", None),
        P(None, "batch", None),
        P(None, "batch", None),
        P("batch"),
        P(None, "batch", None, None),
        P("batch", None, None),
    )
    return jax.shard_map(
        local, mesh=mesh, in_specs=placed, out_specs=P(None, None, "batch", None), check_vma=False
    )
```

```python
import functools

import jax
import jax.numpy as jnp
from jax import lax
from jax.experimental import pallas as pl
from jax.experimental.pallas import tpu as pltpu
from jax.sharding import PartitionSpec as P

MESH = pl.DeviceIdType.MESH
KL = 512
KR = 64
VH = 128
BLOCK = 512
STEPS = 4
NX = 4
LOCAL_HEADS = 4
ROWS = STEPS * LOCAL_HEADS
WIDE = KL + 128
SCALE = (VH + KR) ** (-0.5)
NEG = -1e30
LAST = (((1,), (1,)), ((), ()))
FIRST = (((1,), (0,)), ((), ()))


def mod(value, size):
    return value % size if isinstance(value, int) else lax.rem(value, size)


def div(value, size):
    return value // size if isinstance(value, int) else lax.div(value, size)


def column(x, core):
    source_core = mod(div(x, 2) + core, 2)
    source_x = x + source_core * (NX - 1 - 2 * x)
    request = mod(source_x, 2)
    return request, source_core, source_x


def packed(out, top, total):
    lane = lax.broadcasted_iota(jnp.int32, (out.shape[0], 128), 1)
    high = total.astype(jnp.bfloat16).astype(jnp.float32)
    stats = jnp.where(lane == 0, top, jnp.where(lane == 1, high, jnp.where(lane == 2, total - high, 0.0)))
    return jnp.concatenate([out.astype(jnp.bfloat16), stats.astype(jnp.bfloat16)], axis=1)


def merged(parts, top):
    stats = [part[:, KL:].astype(jnp.float32)[:, :3] for part in parts]
    return joined([part[:, :KL] for part in parts], stats, top)


def joined(values, stats, top):
    for stat in stats:
        top = stat[:, 0:1] if top is None else jnp.maximum(top, stat[:, 0:1])
    out, total = None, None
    for value, stat in zip(values, stats):
        factor = jnp.exp(stat[:, 0:1] - top)
        share = factor * (stat[:, 1:2] + stat[:, 2:3])
        term = factor * value.astype(jnp.float32)
        out = term if out is None else out + term
        total = share if total is None else total + share
    return out, top, total


def kernel(
    n,
    length_hbm, ql_hbm, qr_hbm, sel_hbm, nl_hbm, nr_hbm, lat_hbm, rope_hbm, w_hbm,
    out_ref,
    length_ref, ql_ref, qr_ref, sel_ref, nl_ref, nr_ref, lat, rope, w, rows32, mine, q_all, keep,
    part, part_in, joint, joint_in, done, done_in, final,
    local_sem, q_send, q_recv, x_send, x_recv, px_send, px_recv, py_send, py_recv, back_sem,
    o_send, o_recv,
):
    b, c = lax.axis_index("batch"), lax.axis_index("ctx")
    z, core = div(b, 2), mod(b, 2)
    y, x = div(c, NX), mod(c, NX)
    far = n // 2
    few = max(1, n // 4)
    groups = n // few

    pairs = (
        (ql_hbm, ql_ref), (qr_hbm, qr_ref), (sel_hbm, sel_ref), (nl_hbm, nl_ref), (nr_hbm, nr_ref),
        (length_hbm, length_ref), (lat_hbm, lat), (rope_hbm, rope), (w_hbm, w),
    )
    loads = [pltpu.make_async_copy(src, dst, local_sem.at[k]) for k, (src, dst) in enumerate(pairs)]
    for load in loads:
        load.start()

    def at_y(step):
        return (b, mod(y + step, n) * NX + x)

    def at_x(step):
        return (b, y * NX + mod(x + step + NX, NX))

    request, source_core, source_x = column(x, core)
    own = request * 2 + source_core
    goal_x = x + core * (NX - 1 - 2 * x)
    goal_column = mod(x, 2) * 2 + core
    itself = (y == z) & (div(x, 2) == core) & (goal_x == x)
    other = jnp.logical_not(itself)

    def goal(step):
        return (y * 2 + div(x, 2), mod(y + step, n) * NX + goal_x)

    def origin(step):
        return (mod(z + step, n) * 2 + source_core, z * NX + source_x)

    barrier = pltpu.get_barrier_semaphore()

    def greet(device):
        pl.semaphore_signal(barrier, inc=1, device_id=device, device_id_type=MESH)

    for d in range(1, n):
        greet(goal(d))
        greet(origin(d))
        greet(at_y(d))
    for d in range(1, NX):
        greet(at_x(d))

    @pl.when(other)
    def _():
        greet(goal(0))
        greet(origin(0))

    loads[0].wait()
    loads[1].wait()
    for t in range(STEPS):
        span = pl.ds(t * LOCAL_HEADS, LOCAL_HEADS)
        rows32[span, :KL] = ql_ref[t, 0].astype(jnp.float32)
        rows32[span, KL:KL + KR] = qr_ref[t, 0].astype(jnp.float32)
    rows32[:, KL + KR:] = jnp.zeros((ROWS, WIDE - KL - KR), jnp.float32)
    mine[...] = rows32[...].astype(jnp.bfloat16)

    pl.semaphore_wait(barrier, 3 * (n - 1) + NX - 1 + 2 * other.astype(jnp.int32))

    def remote(src, dst, send, recv, device):
        return pltpu.make_async_remote_copy(
            src_ref=src, dst_ref=dst, send_sem=send, recv_sem=recv, device_id=device, device_id_type=MESH
        )

    def nearest(s):
        return mod(s, 2) * div(s + 1, 2) + (1 - mod(s, 2)) * mod(n - div(s, 2), n)

    def q_copy(d):
        return remote(mine, q_all.at[goal_column, z], q_send.at[d], q_recv.at[z], goal(d))

    def q_wait(k):
        slot = q_all.at[own, k]
        remote(slot, slot, q_send.at[0], q_recv.at[k], goal(0)).wait_recv()

    for s in range(1, n):
        q_copy(nearest(n - s)).start()

    @pl.when(other)
    def _():
        q_copy(0).start()

    @pl.when(itself)
    def _():
        q_all[own, z] = mine[...]

    tall = n * ROWS
    row = lax.broadcasted_iota(jnp.int32, (tall, n), 0)
    group = lax.broadcasted_iota(jnp.int32, (tall, n), 1)
    spread = jnp.where(group == row // ROWS, 1.0, 0.0).astype(jnp.bfloat16)
    loads[2].wait()
    hits = []
    for t in range(STEPS):
        chosen = sel_ref[t]
        for k in range(2):
            hits.append(jnp.max(jnp.where(chosen == c * 2 + k, 1.0, 0.0), axis=0))
    table = jnp.concatenate(hits, axis=0).astype(jnp.bfloat16)
    marks = lax.dot_general(spread, table, LAST, preferred_element_type=jnp.float32)
    lane = lax.broadcasted_iota(jnp.int32, (tall, STEPS * 4), 1)
    step = lax.broadcasted_iota(jnp.int32, (tall, STEPS * 4), 0) % ROWS // LOCAL_HEADS
    marks = jnp.where(lane // 4 == step, marks, 0.0).astype(jnp.bfloat16)
    source = lax.broadcasted_iota(jnp.int32, (STEPS * 4, 128), 0) % 4
    target = lax.broadcasted_iota(jnp.int32, (STEPS * 4, 128), 1)
    for r in range(2):
        pick = jnp.where((target < 2) & (source == target * 2 + r), 1.0, 0.0).astype(jnp.bfloat16)
        kept = lax.dot_general(marks, pick, FIRST, preferred_element_type=jnp.float32)
        keep[r] = kept.reshape(n, ROWS, 128)

    def x_copy(d, k):
        slot = q_all.at[own, k]
        return remote(slot, slot, x_send.at[d - 1, k], x_recv.at[d - 1, k], at_x(d))

    @pl.loop(0, n)
    def _(k):

        @pl.when((k != z) | other)
        def _():
            q_wait(k)

        for d in (1, 3, 2):
            x_copy(d, k).start()

    for load in loads[3:8]:
        load.wait()

    def px_copy(d, half):
        target = column(mod(x - d + NX, NX), core)
        return remote(
            part.at[half, target[0] * 2 + target[1]], part_in.at[half, d - 1],
            px_send.at[d - 1, half], px_recv.at[d - 1, half], at_x(-d),
        )

    rows = 2 * few * ROWS
    lane = lax.broadcasted_iota(jnp.int32, (ROWS, 128), 1)

    @pl.loop(0, 2 * groups)
    def _(turn):
        half = div(turn, 2)
        r = mod(request + 1 + turn, 2)
        request_x = 2 * core + r
        away = [mod(x - request_x - k * (NX - 1 - 2 * request_x) + 2 * NX, NX) for k in range(2)]
        for d in away:
            @pl.when(d > 0)
            def _():
                @pl.loop(half * few, half * few + few)
                def _(k):
                    x_copy(d, k).wait_recv()

        span = pl.ds(half * few, few)
        query = q_all[pl.ds(r * 2, 2), span].reshape(rows, WIDE)
        scores = lax.dot_general(query[:, :KL], lat[r], LAST, preferred_element_type=jnp.float32)
        scores = scores + lax.dot_general(
            query[:, KL:KL + KR], rope[r], FIRST, preferred_element_type=jnp.float32
        )
        scores = scores * SCALE
        length = length_ref[r]
        hits = keep[r, span].reshape(rows // 2, 128)
        hits = jnp.concatenate([hits, hits], axis=0)
        place = lax.broadcasted_iota(jnp.int32, (rows, BLOCK), 1)
        masks, masked = [], []
        for k in range(2):
            mask = (hits[:, k:k + 1] > 0.5) & (place + (c * 2 + k) * BLOCK < length)
            masks.append(mask)
            masked.append(jnp.where(mask, scores[:, k * BLOCK:(k + 1) * BLOCK], NEG))
        top = jnp.maximum(
            jnp.max(masked[0], axis=1, keepdims=True), jnp.max(masked[1], axis=1, keepdims=True)
        )
        top = top.astype(jnp.bfloat16).astype(jnp.float32)
        weights = [jnp.where(m, jnp.exp(v - top), 0.0) for m, v in zip(masks, masked)]
        total = jnp.sum(weights[0], axis=1, keepdims=True) + jnp.sum(weights[1], axis=1, keepdims=True)
        rounded = jnp.concatenate([v.astype(jnp.bfloat16) for v in weights], axis=1)
        out = lax.dot_general(rounded, lat[r], FIRST, preferred_element_type=jnp.float32)
        out = out.astype(jnp.bfloat16)
        high = total.astype(jnp.bfloat16).astype(jnp.float32)
        low = total - high
        for k in range(2):
            stats = jnp.zeros((ROWS, 128), jnp.float32)
            for j in range(few):
                at = slice((k * few + j) * ROWS, (k * few + j + 1) * ROWS)
                part[half, r * 2 + k, :, j * KL:(j + 1) * KL] = out[at]
                for m, term in enumerate((top, high, low)):
                    stats = jnp.where(lane == 3 * j + m, term[at], stats)
            part[half, r * 2 + k, :, few * KL:] = stats.astype(jnp.bfloat16)
        for d in away:
            @pl.when(d > 0)
            def _():
                px_copy(d, half).start()

    mine_k = mod(y + far, n)
    q_own = q_all[own, mine_k].astype(jnp.float32)
    row_step = lax.broadcasted_iota(jnp.int32, (ROWS, 1), 0) // LOCAL_HEADS
    second = request.astype(jnp.float32)
    new_rows, new_scores = [], []
    for u in range(STEPS):
        both = nl_ref[u].astype(jnp.float32)
        both_rope = nr_ref[u].astype(jnp.float32)
        new_row = both[0:1] * (1.0 - second) + both[1:2] * second
        new_rope = both_rope[0:1] * (1.0 - second) + both_rope[1:2] * second
        score = jnp.sum(q_own[:, :KL] * new_row, axis=1, keepdims=True)
        score = (score + jnp.sum(q_own[:, KL:KL + KR] * new_rope, axis=1, keepdims=True)) * SCALE
        new_rows.append(new_row)
        new_scores.append(jnp.where(row_step >= u, score, NEG))
    new_top = new_scores[0]
    for score in new_scores[1:]:
        new_top = jnp.maximum(new_top, score)

    def py_copy(k):
        to = mod(k + far, n)
        return remote(joint.at[k], joint_in.at[y], py_send.at[k], py_recv.at[y], (b, to * NX + x))

    @pl.loop(0, groups)
    def _(half):
        for d in (1, 3, 2):
            px_copy(d, half).wait_recv()
        stats = [part[half, own, :, few * KL:].astype(jnp.float32)]
        stats += [part_in[half, e, :, few * KL:].astype(jnp.float32) for e in range(NX - 1)]
        for j in range(few):
            at = slice(j * KL, (j + 1) * KL)
            values = [part[half, own, :, at]] + [part_in[half, e, :, at] for e in range(NX - 1)]
            three = [stat[:, 3 * j:3 * j + 3] for stat in stats]
            k = half * few + j
            joint[k] = packed(*joined(values, three, None))

            @pl.when(k != mine_k)
            def _():
                py_copy(k).start()

    joint_in[y] = joint[mine_k]

    @pl.loop(1, n)
    def _(d):
        k = mod(y + d, n)
        remote(joint.at[0], joint_in.at[k], py_send.at[0], py_recv.at[k], at_y(d)).wait_recv()

    out, top, total = merged([joint_in[k] for k in range(n)], new_top)
    for u in range(STEPS):
        weight = jnp.where(row_step >= u, jnp.exp(new_scores[u] - top), 0.0)
        total = total + weight
        out = out + weight.astype(jnp.bfloat16).astype(jnp.float32) * new_rows[u]
    done[...] = out / total

    back = remote(done, done_in, back_sem.at[0], back_sem.at[1], origin(mod(mine_k - z + n, n)))
    back.start()

    @pl.loop(1, n)
    def _(d):
        q_copy(d).wait_send()
        py_copy(mod(mine_k + d, n)).wait_send()

    @pl.when(other)
    def _():
        q_copy(0).wait_send()

    @pl.loop(1, NX)
    def _(d):
        for half in range(groups):
            px_copy(d, half).wait_send()

        @pl.loop(0, n)
        def _(k):
            x_copy(d, k).wait_send()

    loads[8].wait()
    back.wait_recv()
    value = done_in[...]

    high = value.astype(jnp.bfloat16)
    rest = value - high.astype(jnp.float32)
    middle = rest.astype(jnp.bfloat16)
    low = (rest - middle.astype(jnp.float32)).astype(jnp.bfloat16)
    terms = jnp.concatenate([high, middle, low], axis=0)
    row_head = lax.broadcasted_iota(jnp.int32, (ROWS, VH), 0) % LOCAL_HEADS
    result = jnp.zeros((ROWS, VH), jnp.float32)
    for h in range(LOCAL_HEADS):
        product = lax.dot_general(terms, w[h], FIRST, preferred_element_type=jnp.float32)
        product = product[:ROWS] + (product[ROWS:2 * ROWS] + product[2 * ROWS:])
        result = jnp.where(row_head == h, product, result)
    final[...] = result.astype(jnp.bfloat16)

    def o_copy(dy, dx):
        target = (b, mod(y + dy, n) * NX + mod(x + dx, NX))
        return remote(final, out_ref.at[x, y], o_send.at[dx, dy], o_recv.at[dx, dy], target)

    @pl.loop(0, n - 1)
    def _(s):
        dy = nearest(n - 1 - s)
        for dx in (2, 1, 3, 0):
            o_copy(dy, dx).start()

    for dx in (2, 1, 3):
        o_copy(0, dx).start()
    keep_own = pltpu.make_async_copy(final, out_ref.at[x, y], local_sem.at[9])
    keep_own.start()

    back.wait_send()

    @pl.loop(1, n * NX)
    def _(k):
        o_copy(div(k, NX), mod(k, NX)).wait_send()

    @pl.loop(1, n * NX)
    def _(k):
        o_copy(div(k, NX), mod(k, NX)).wait_recv()

    keep_own.wait()


def local(
    q_latent, q_rope, cache_latent, cache_rope, new_latent, new_rope, lengths, selected, w_uv
):
    n = lax.axis_size("ctx") // NX
    selected = jnp.transpose(selected, (0, 3, 1, 2))
    cache_rope = jnp.swapaxes(cache_rope, 1, 2)
    held = cache_latent.shape[1]
    few = max(1, n // 4)
    bf16, f32 = jnp.bfloat16, jnp.float32
    dma = pltpu.SemaphoreType.DMA
    anywhere = pl.BlockSpec(memory_space=pl.ANY)
    out = pl.pallas_call(
        functools.partial(kernel, n),
        out_shape=jax.ShapeDtypeStruct((NX, n, ROWS, VH), bf16),
        in_specs=[anywhere] * 9,
        out_specs=anywhere,
        scratch_shapes=[
            pltpu.SMEM((2,), jnp.int32),
            pltpu.VMEM(q_latent.shape, bf16),
            pltpu.VMEM(q_rope.shape, bf16),
            pltpu.VMEM(selected.shape, jnp.int32),
            pltpu.VMEM(new_latent.shape, bf16),
            pltpu.VMEM(new_rope.shape, bf16),
            pltpu.VMEM((2, held, KL), bf16),
            pltpu.VMEM((2, KR, held), bf16),
            pltpu.VMEM((LOCAL_HEADS, KL, VH), bf16),
            pltpu.VMEM((ROWS, WIDE), f32),
            pltpu.VMEM((ROWS, WIDE), bf16),
            pltpu.VMEM((NX, n, ROWS, WIDE), bf16),
            pltpu.VMEM((2, n, ROWS, 128), f32),
            pltpu.VMEM((n // few, NX, ROWS, few * KL + 128), bf16),
            pltpu.VMEM((n // few, NX - 1, ROWS, few * KL + 128), bf16),
            pltpu.VMEM((n, ROWS, WIDE), bf16),
            pltpu.VMEM((n, ROWS, WIDE), bf16),
            pltpu.VMEM((ROWS, KL), f32),
            pltpu.VMEM((ROWS, KL), f32),
            pltpu.VMEM((ROWS, VH), bf16),
            dma((10,)),
            dma((n,)), dma((n,)),
            dma((NX - 1, n)), dma((NX - 1, n)),
            dma((NX - 1, n // few)), dma((NX - 1, n // few)),
            dma((n,)), dma((n,)),
            dma((2,)),
            dma((NX, n)), dma((NX, n)),
        ],
        compiler_params=pltpu.CompilerParams(
            collective_id=0, has_side_effects=True, vmem_limit_bytes=60 * 1024 * 1024
        ),
    )(lengths, q_latent, q_rope, selected, new_latent, new_rope, cache_latent, cache_rope, w_uv)
    out = out.reshape(NX, n, STEPS, LOCAL_HEADS, VH)
    return jnp.transpose(out, (2, 1, 0, 3, 4)).reshape(STEPS, NX * n, LOCAL_HEADS, VH)


def solution(mesh):
    placed = (
        P(None, "ctx", "batch", None),
        P(None, "ctx", "batch", None),
        P("batch", "ctx", None),
        P("batch", "ctx", None),
        P(None, "batch", None),
        P(None, "batch", None),
        P("batch"),
        P(None, "batch", None, None),
        P("batch", None, None),
    )
    return jax.shard_map(
        local, mesh=mesh, in_specs=placed, out_specs=P(None, None, "batch", None), check_vma=False
    )
```

```python
import functools

import jax
import jax.numpy as jnp
from jax import lax
from jax.experimental import pallas as pl
from jax.experimental.pallas import tpu as pltpu
from jax.sharding import PartitionSpec as P

MESH = pl.DeviceIdType.MESH
KL = 512
KR = 64
VH = 128
BLOCK = 512
STEPS = 4
NX = 4
LOCAL_HEADS = 4
ROWS = STEPS * LOCAL_HEADS
WIDE = KL + 128
SCALE = (VH + KR) ** (-0.5)
NEG = -1e30
LAST = (((1,), (1,)), ((), ()))
FIRST = (((1,), (0,)), ((), ()))


def mod(value, size):
    return value % size if isinstance(value, int) else lax.rem(value, size)


def div(value, size):
    return value // size if isinstance(value, int) else lax.div(value, size)


def column(x, core):
    source_core = mod(div(x, 2) + core, 2)
    source_x = x + source_core * (NX - 1 - 2 * x)
    request = mod(source_x, 2)
    return request, source_core, source_x


def packed(out, top, total):
    lane = lax.broadcasted_iota(jnp.int32, (out.shape[0], 128), 1)
    high = total.astype(jnp.bfloat16).astype(jnp.float32)
    stats = jnp.where(lane == 0, top, jnp.where(lane == 1, high, jnp.where(lane == 2, total - high, 0.0)))
    return jnp.concatenate([out.astype(jnp.bfloat16), stats.astype(jnp.bfloat16)], axis=1)


def merged(parts, top):
    stats = [part[:, KL:].astype(jnp.float32)[:, :3] for part in parts]
    return joined([part[:, :KL] for part in parts], stats, top)


def joined(values, stats, top):
    for stat in stats:
        top = stat[:, 0:1] if top is None else jnp.maximum(top, stat[:, 0:1])
    out, total = None, None
    for value, stat in zip(values, stats):
        factor = jnp.exp(stat[:, 0:1] - top)
        share = factor * (stat[:, 1:2] + stat[:, 2:3])
        term = factor * value.astype(jnp.float32)
        out = term if out is None else out + term
        total = share if total is None else total + share
    return out, top, total


def kernel(
    n,
    length_hbm, ql_hbm, qr_hbm, sel_hbm, nl_hbm, nr_hbm, lat_hbm, rope_hbm, w_hbm,
    out_ref,
    length_ref, ql_ref, qr_ref, sel_ref, nl_ref, nr_ref, lat, rope, w, rows32, mine, q_all, keep,
    part, part_in, joint, joint_in, done, done_in, final,
    local_sem, q_send, q_recv, x_send, x_recv, px_send, px_recv, py_send, py_recv, back_sem,
    o_send, o_recv,
):
    b, c = lax.axis_index("batch"), lax.axis_index("ctx")
    z, core = div(b, 2), mod(b, 2)
    y, x = div(c, NX), mod(c, NX)
    far = n // 2
    few = max(1, n // 4)
    groups = n // few

    pairs = (
        (ql_hbm, ql_ref), (qr_hbm, qr_ref), (sel_hbm, sel_ref), (nl_hbm, nl_ref), (nr_hbm, nr_ref),
        (length_hbm, length_ref), (lat_hbm, lat), (rope_hbm, rope), (w_hbm, w),
    )
    loads = [pltpu.make_async_copy(src, dst, local_sem.at[k]) for k, (src, dst) in enumerate(pairs)]
    for load in loads:
        load.start()

    def at_y(step):
        return (b, mod(y + step, n) * NX + x)

    def at_x(step):
        return (b, y * NX + mod(x + step + NX, NX))

    request, source_core, source_x = column(x, core)
    own = request * 2 + source_core
    goal_x = x + core * (NX - 1 - 2 * x)
    goal_column = mod(x, 2) * 2 + core
    itself = (y == z) & (div(x, 2) == core) & (goal_x == x)
    other = jnp.logical_not(itself)

    def goal(step):
        return (y * 2 + div(x, 2), mod(y + step, n) * NX + goal_x)

    def origin(step):
        return (mod(z + step, n) * 2 + source_core, z * NX + source_x)

    barrier = pltpu.get_barrier_semaphore()

    def greet(device):
        pl.semaphore_signal(barrier, inc=1, device_id=device, device_id_type=MESH)

    for d in range(1, n):
        greet(goal(d))
        greet(origin(d))
        greet(at_y(d))
    for d in range(1, NX):
        greet(at_x(d))

    @pl.when(other)
    def _():
        greet(goal(0))
        greet(origin(0))

    loads[0].wait()
    loads[1].wait()
    for t in range(STEPS):
        span = pl.ds(t * LOCAL_HEADS, LOCAL_HEADS)
        rows32[span, :KL] = ql_ref[t, 0].astype(jnp.float32)
        rows32[span, KL:KL + KR] = qr_ref[t, 0].astype(jnp.float32)
    rows32[:, KL + KR:] = jnp.zeros((ROWS, WIDE - KL - KR), jnp.float32)
    mine[...] = rows32[...].astype(jnp.bfloat16)

    pl.semaphore_wait(barrier, 3 * (n - 1) + NX - 1 + 2 * other.astype(jnp.int32))

    def remote(src, dst, send, recv, device):
        return pltpu.make_async_remote_copy(
            src_ref=src, dst_ref=dst, send_sem=send, recv_sem=recv, device_id=device, device_id_type=MESH
        )

    def nearest(s):
        return mod(s, 2) * div(s + 1, 2) + (1 - mod(s, 2)) * mod(n - div(s, 2), n)

    def q_copy(d):
        return remote(mine, q_all.at[goal_column, z], q_send.at[d], q_recv.at[z], goal(d))

    def q_wait(k):
        slot = q_all.at[own, k]
        remote(slot, slot, q_send.at[0], q_recv.at[k], goal(0)).wait_recv()

    for s in range(1, n):
        q_copy(nearest(n - s)).start()

    @pl.when(other)
    def _():
        q_copy(0).start()

    @pl.when(itself)
    def _():
        q_all[own, z] = mine[...]

    tall = n * ROWS
    row = lax.broadcasted_iota(jnp.int32, (tall, n), 0)
    group = lax.broadcasted_iota(jnp.int32, (tall, n), 1)
    spread = jnp.where(group == row // ROWS, 1.0, 0.0).astype(jnp.bfloat16)
    loads[2].wait()
    hits = []
    for t in range(STEPS):
        chosen = sel_ref[t]
        for k in range(2):
            hits.append(jnp.max(jnp.where(chosen == c * 2 + k, 1.0, 0.0), axis=0))
    table = jnp.concatenate(hits, axis=0).astype(jnp.bfloat16)
    marks = lax.dot_general(spread, table, LAST, preferred_element_type=jnp.float32)
    lane = lax.broadcasted_iota(jnp.int32, (tall, STEPS * 4), 1)
    step = lax.broadcasted_iota(jnp.int32, (tall, STEPS * 4), 0) % ROWS // LOCAL_HEADS
    marks = jnp.where(lane // 4 == step, marks, 0.0).astype(jnp.bfloat16)
    source = lax.broadcasted_iota(jnp.int32, (STEPS * 4, 128), 0) % 4
    target = lax.broadcasted_iota(jnp.int32, (STEPS * 4, 128), 1)
    for r in range(2):
        pick = jnp.where((target < 2) & (source == target * 2 + r), 1.0, 0.0).astype(jnp.bfloat16)
        kept = lax.dot_general(marks, pick, FIRST, preferred_element_type=jnp.float32)
        keep[r] = kept.reshape(n, ROWS, 128)

    def x_copy(d, k):
        slot = q_all.at[own, k]
        return remote(slot, slot, x_send.at[d - 1, k], x_recv.at[d - 1, k], at_x(d))

    @pl.loop(0, n)
    def _(k):

        @pl.when((k != z) | other)
        def _():
            q_wait(k)

        for d in (1, 3, 2):
            x_copy(d, k).start()

    for load in loads[3:8]:
        load.wait()

    def px_copy(d, half):
        target = column(mod(x - d + NX, NX), core)
        return remote(
            part.at[half, target[0] * 2 + target[1]], part_in.at[half, d - 1],
            px_send.at[d - 1, half], px_recv.at[d - 1, half], at_x(-d),
        )

    rows = 2 * few * ROWS
    lane = lax.broadcasted_iota(jnp.int32, (ROWS, 128), 1)

    @pl.loop(0, 2 * groups)
    def _(turn):
        half = div(turn, 2)
        r = mod(request + 1 + turn, 2)
        request_x = 2 * core + r
        away = [mod(x - request_x - k * (NX - 1 - 2 * request_x) + 2 * NX, NX) for k in range(2)]
        for d in away:
            @pl.when(d > 0)
            def _():
                @pl.loop(half * few, half * few + few)
                def _(k):
                    x_copy(d, k).wait_recv()

        span = pl.ds(half * few, few)
        query = q_all[pl.ds(r * 2, 2), span].reshape(rows, WIDE)
        scores = lax.dot_general(query[:, :KL], lat[r], LAST, preferred_element_type=jnp.float32)
        scores = scores + lax.dot_general(
            query[:, KL:KL + KR], rope[r], FIRST, preferred_element_type=jnp.float32
        )
        scores = scores * SCALE
        length = length_ref[r]
        hits = keep[r, span].reshape(rows // 2, 128)
        hits = jnp.concatenate([hits, hits], axis=0)
        place = lax.broadcasted_iota(jnp.int32, (rows, BLOCK), 1)
        masks, masked = [], []
        for k in range(2):
            mask = (hits[:, k:k + 1] > 0.5) & (place + (c * 2 + k) * BLOCK < length)
            masks.append(mask)
            masked.append(jnp.where(mask, scores[:, k * BLOCK:(k + 1) * BLOCK], NEG))
        top = jnp.maximum(
            jnp.max(masked[0], axis=1, keepdims=True), jnp.max(masked[1], axis=1, keepdims=True)
        )
        top = top.astype(jnp.bfloat16).astype(jnp.float32)
        weights = [jnp.where(m, jnp.exp(v - top), 0.0) for m, v in zip(masks, masked)]
        total = jnp.sum(weights[0], axis=1, keepdims=True) + jnp.sum(weights[1], axis=1, keepdims=True)
        rounded = jnp.concatenate([v.astype(jnp.bfloat16) for v in weights], axis=1)
        out = lax.dot_general(rounded, lat[r], FIRST, preferred_element_type=jnp.float32)
        out = out.astype(jnp.bfloat16)
        high = total.astype(jnp.bfloat16).astype(jnp.float32)
        low = total - high
        for k in range(2):
            stats = jnp.zeros((ROWS, 128), jnp.float32)
            for j in range(few):
                at = slice((k * few + j) * ROWS, (k * few + j + 1) * ROWS)
                part[half, r * 2 + k, :, j * KL:(j + 1) * KL] = out[at]
                for m, term in enumerate((top, high, low)):
                    stats = jnp.where(lane == 3 * j + m, term[at], stats)
            part[half, r * 2 + k, :, few * KL:] = stats.astype(jnp.bfloat16)
        for d in away:
            @pl.when(d > 0)
            def _():
                px_copy(d, half).start()

    mine_k = mod(y + far, n)
    q_own = q_all[own, mine_k].astype(jnp.float32)
    row_step = lax.broadcasted_iota(jnp.int32, (ROWS, 1), 0) // LOCAL_HEADS
    second = request.astype(jnp.float32)
    new_rows, new_scores = [], []
    for u in range(STEPS):
        both = nl_ref[u].astype(jnp.float32)
        both_rope = nr_ref[u].astype(jnp.float32)
        new_row = both[0:1] * (1.0 - second) + both[1:2] * second
        new_rope = both_rope[0:1] * (1.0 - second) + both_rope[1:2] * second
        score = jnp.sum(q_own[:, :KL] * new_row, axis=1, keepdims=True)
        score = (score + jnp.sum(q_own[:, KL:KL + KR] * new_rope, axis=1, keepdims=True)) * SCALE
        new_rows.append(new_row)
        new_scores.append(jnp.where(row_step >= u, score, NEG))
    new_top = new_scores[0]
    for score in new_scores[1:]:
        new_top = jnp.maximum(new_top, score)

    def py_copy(k):
        to = mod(k + far, n)
        return remote(joint.at[k], joint_in.at[y], py_send.at[k], py_recv.at[y], (b, to * NX + x))

    @pl.loop(0, groups)
    def _(half):
        for d in (1, 3, 2):
            px_copy(d, half).wait_recv()
        stats = [part[half, own, :, few * KL:].astype(jnp.float32)]
        stats += [part_in[half, e, :, few * KL:].astype(jnp.float32) for e in range(NX - 1)]
        for j in range(few):
            at = slice(j * KL, (j + 1) * KL)
            values = [part[half, own, :, at]] + [part_in[half, e, :, at] for e in range(NX - 1)]
            three = [stat[:, 3 * j:3 * j + 3] for stat in stats]
            k = half * few + j
            joint[k] = packed(*joined(values, three, None))

        @pl.loop(0, few)
        def _(j):
            k = half * few + mod(j + y, few)

            @pl.when(k != mine_k)
            def _():
                py_copy(k).start()

    joint_in[y] = joint[mine_k]

    @pl.loop(1, n)
    def _(d):
        k = mod(y + d, n)
        remote(joint.at[0], joint_in.at[k], py_send.at[0], py_recv.at[k], at_y(d)).wait_recv()

    out, top, total = merged([joint_in[k] for k in range(n)], new_top)
    for u in range(STEPS):
        weight = jnp.where(row_step >= u, jnp.exp(new_scores[u] - top), 0.0)
        total = total + weight
        out = out + weight.astype(jnp.bfloat16).astype(jnp.float32) * new_rows[u]
    done[...] = out / total

    back = remote(done, done_in, back_sem.at[0], back_sem.at[1], origin(mod(mine_k - z + n, n)))
    back.start()

    @pl.loop(1, n)
    def _(d):
        q_copy(d).wait_send()
        py_copy(mod(mine_k + d, n)).wait_send()

    @pl.when(other)
    def _():
        q_copy(0).wait_send()

    @pl.loop(1, NX)
    def _(d):
        for half in range(groups):
            px_copy(d, half).wait_send()

        @pl.loop(0, n)
        def _(k):
            x_copy(d, k).wait_send()

    loads[8].wait()
    back.wait_recv()
    value = done_in[...]

    high = value.astype(jnp.bfloat16)
    rest = value - high.astype(jnp.float32)
    middle = rest.astype(jnp.bfloat16)
    low = (rest - middle.astype(jnp.float32)).astype(jnp.bfloat16)
    terms = jnp.concatenate([high, middle, low], axis=0)
    row_head = lax.broadcasted_iota(jnp.int32, (ROWS, VH), 0) % LOCAL_HEADS
    result = jnp.zeros((ROWS, VH), jnp.float32)
    for h in range(LOCAL_HEADS):
        product = lax.dot_general(terms, w[h], FIRST, preferred_element_type=jnp.float32)
        product = product[:ROWS] + (product[ROWS:2 * ROWS] + product[2 * ROWS:])
        result = jnp.where(row_head == h, product, result)
    final[...] = result.astype(jnp.bfloat16)

    def o_copy(dy, dx):
        target = (b, mod(y + dy, n) * NX + mod(x + dx, NX))
        return remote(final, out_ref.at[x, y], o_send.at[dx, dy], o_recv.at[dx, dy], target)

    @pl.loop(0, n - 1)
    def _(s):
        dy = nearest(n - 1 - s)
        for dx in (2, 1, 3, 0):
            o_copy(dy, dx).start()

    for dx in (2, 1, 3):
        o_copy(0, dx).start()
    keep_own = pltpu.make_async_copy(final, out_ref.at[x, y], local_sem.at[9])
    keep_own.start()

    back.wait_send()

    @pl.loop(1, n * NX)
    def _(k):
        o_copy(div(k, NX), mod(k, NX)).wait_send()

    @pl.loop(1, n * NX)
    def _(k):
        o_copy(div(k, NX), mod(k, NX)).wait_recv()

    keep_own.wait()


def local(
    q_latent, q_rope, cache_latent, cache_rope, new_latent, new_rope, lengths, selected, w_uv
):
    n = lax.axis_size("ctx") // NX
    selected = jnp.transpose(selected, (0, 3, 1, 2))
    cache_rope = jnp.swapaxes(cache_rope, 1, 2)
    held = cache_latent.shape[1]
    few = max(1, n // 4)
    bf16, f32 = jnp.bfloat16, jnp.float32
    dma = pltpu.SemaphoreType.DMA
    anywhere = pl.BlockSpec(memory_space=pl.ANY)
    out = pl.pallas_call(
        functools.partial(kernel, n),
        out_shape=jax.ShapeDtypeStruct((NX, n, ROWS, VH), bf16),
        in_specs=[anywhere] * 9,
        out_specs=anywhere,
        scratch_shapes=[
            pltpu.SMEM((2,), jnp.int32),
            pltpu.VMEM(q_latent.shape, bf16),
            pltpu.VMEM(q_rope.shape, bf16),
            pltpu.VMEM(selected.shape, jnp.int32),
            pltpu.VMEM(new_latent.shape, bf16),
            pltpu.VMEM(new_rope.shape, bf16),
            pltpu.VMEM((2, held, KL), bf16),
            pltpu.VMEM((2, KR, held), bf16),
            pltpu.VMEM((LOCAL_HEADS, KL, VH), bf16),
            pltpu.VMEM((ROWS, WIDE), f32),
            pltpu.VMEM((ROWS, WIDE), bf16),
            pltpu.VMEM((NX, n, ROWS, WIDE), bf16),
            pltpu.VMEM((2, n, ROWS, 128), f32),
            pltpu.VMEM((n // few, NX, ROWS, few * KL + 128), bf16),
            pltpu.VMEM((n // few, NX - 1, ROWS, few * KL + 128), bf16),
            pltpu.VMEM((n, ROWS, WIDE), bf16),
            pltpu.VMEM((n, ROWS, WIDE), bf16),
            pltpu.VMEM((ROWS, KL), f32),
            pltpu.VMEM((ROWS, KL), f32),
            pltpu.VMEM((ROWS, VH), bf16),
            dma((10,)),
            dma((n,)), dma((n,)),
            dma((NX - 1, n)), dma((NX - 1, n)),
            dma((NX - 1, n // few)), dma((NX - 1, n // few)),
            dma((n,)), dma((n,)),
            dma((2,)),
            dma((NX, n)), dma((NX, n)),
        ],
        compiler_params=pltpu.CompilerParams(
            collective_id=0, has_side_effects=True, vmem_limit_bytes=60 * 1024 * 1024
        ),
    )(lengths, q_latent, q_rope, selected, new_latent, new_rope, cache_latent, cache_rope, w_uv)
    out = out.reshape(NX, n, STEPS, LOCAL_HEADS, VH)
    return jnp.transpose(out, (2, 1, 0, 3, 4)).reshape(STEPS, NX * n, LOCAL_HEADS, VH)


def solution(mesh):
    placed = (
        P(None, "ctx", "batch", None),
        P(None, "ctx", "batch", None),
        P("batch", "ctx", None),
        P("batch", "ctx", None),
        P(None, "batch", None),
        P(None, "batch", None),
        P("batch"),
        P(None, "batch", None, None),
        P("batch", None, None),
    )
    return jax.shard_map(
        local, mesh=mesh, in_specs=placed, out_specs=P(None, None, "batch", None), check_vma=False
    )
```
